32 devices in a mesh: space: 16 (over z, y, core), bead: 2 (over x).
Axes of the slice: x: 2, y: 2, z: 4, core: 2. Of those that a mesh axis runs over, the one named last changes fastest.
Arguments:
- positions: float32 [8, 3, 1536], P('bead', None, 'space'), may hold values from -6 to 6
- momenta: float32 [8, 3, 1536], P('bead', None, 'space'), may hold values from -6 to 6
- neighbours: int32 [1536, 64], P('space'), may hold values from 0 to 479, as said below
- nbr_count: int32 [1536], P('space'), may hold values from 32 to 64
- send_rows: int32 [16, 4, 96], P('space'), may hold values from -1 to 95, as said below
- embed_first: float32 [2, 128], replicated, may hold values from -6 to 6
- embed_weight: bfloat16 [128, 128], replicated, may hold values from -0.5 to 0.5
- embed_bias: float32 [128], replicated, may hold values from -3 to 3
- fit_weight: bfloat16 [2048, 240], replicated, may hold values from -0.125 to 0.125
- fit_bias: float32 [240], replicated, may hold values from -3 to 3
- fit_weight2: bfloat16 [240, 240], replicated, may hold values from -0.375 to 0.375
- fit_bias2: float32 [240], replicated, may hold values from -3 to 3
- fit_out: float32 [240], replicated, may hold values from -0.375 to 0.375
Outputs:
- new_positions: float32 [8, 3, 1536], P('bead', None, 'space')
- new_momenta: float32 [8, 3, 1536], P('bead', None, 'space')
The draws below stay inside these ranges and needn't reach their ends.
Inputs may be any that keep to these rules, and one draw needn't show every extreme that they name: `neighbours`: an entry below 96 names another own atom of the domain; an entry 96 + j * 96 + s names ghost slot s of block j, and that slot holds an atom. Entries past nbr_count are padding of the same kind. `send_rows`: -1 marks an empty slot. In each block the filled slots come first and name distinct atoms; blocks toward a domain that does not exist are empty; in every draw some block is full.
All inputs are finite; a program needn't handle non-finite values.
Results may differ from the reference program's by a relative error of at most 0.03.
Values sent between devices are 32-bit elements; how exact they have to be, the bound alone decides.
No kernel may reach another device: no remote copies, remote signals or barrier semaphores. Data moves between devices by JAX's collectives and lax.ppermute only.
A program may use at most 64 MiB of HBM per device.

```python
import jax
import jax.numpy as jnp
import numpy as np
from jax import lax

ATOMS_DEV = 96
REACH = 2
NBR = 64
EMB = 128
AXIS = 16
FIT = 240
GSLOT = 96
DOMAINS = 16
ATOMS = 1536
BEADS = 8


def ghost_layout(key):
    base_key = jax.random.fold_in(key, 101)
    key_list = jax.random.split(base_key, DOMAINS * 2 * REACH)

    def one_order(single_key):
        return jax.random.permutation(single_key, ATOMS_DEV)
    orders = jax.vmap(one_order)(key_list).reshape(DOMAINS, 2 * REACH, ATOMS_DEV)[:, :, :GSLOT]
    counts = jax.random.randint(jax.random.fold_in(key, 102), (DOMAINS, 2 * REACH), GSLOT // 4, GSLOT + 1)
    block_ids = jnp.arange(2 * REACH)
    domain = jnp.arange(DOMAINS)
    counts = jnp.where(block_ids[None, :] == (domain % (2 * REACH))[:, None], GSLOT, counts)
    offsets = jnp.concatenate([jnp.arange(-REACH, 0), jnp.arange(1, REACH + 1)])
    target = domain[:, None] + offsets[None, :]
    counts = jnp.where((target >= 0) & (target < DOMAINS), counts, 0)
    slot_ids = jnp.arange(GSLOT)
    row_table = jnp.where(slot_ids[None, None, :] < counts[:, :, None], orders, -1)
    return (row_table.astype(jnp.int32), counts.astype(jnp.int32))


def draw_send_rows(key, part):
    row_table, counts = ghost_layout(key)
    return row_table


def draw_neighbours(key, part):
    row_table, counts = ghost_layout(key)
    key = jax.random.fold_in(key, 3)
    offsets = jnp.concatenate([jnp.arange(-REACH, 0), jnp.arange(1, REACH + 1)])
    domain = jnp.arange(DOMAINS)
    block_ids = jnp.arange(2 * REACH)
    source = domain[:, None] - offsets[None, :]
    inside = (source >= 0) & (source < DOMAINS)
    incoming = jnp.where(inside, counts[jnp.clip(source, 0, DOMAINS - 1), block_ids[None, :]], 0)
    first_key, second_key, third_key = jax.random.split(key, 3)
    shape = (DOMAINS, ATOMS_DEV, NBR)
    chosen = jax.random.randint(first_key, shape, 0, 2 * REACH + 2)
    blocks = jnp.clip(chosen, 0, 2 * REACH - 1)
    avail = incoming[domain[:, None, None], blocks]
    is_ghost = (chosen < 2 * REACH) & (avail > 0)
    slot_pick = jax.random.randint(second_key, shape, 0, jnp.maximum(avail, 1))
    atom_ids = jnp.arange(ATOMS_DEV)[None, :, None]
    own_pick = (atom_ids + 1 + jax.random.randint(third_key, shape, 0, ATOMS_DEV - 1)) % ATOMS_DEV
    local_ids = jnp.where(is_ghost, ATOMS_DEV + blocks * GSLOT + slot_pick, own_pick)
    return local_ids.reshape(DOMAINS * ATOMS_DEV, NBR).astype(jnp.int32)


def draw_nbr_count(key, part):
    key = jax.random.fold_in(key, 7)
    counts = jax.random.randint(key, (DOMAINS * ATOMS_DEV,), NBR // 2, NBR + 1)
    counts = jnp.where(jnp.arange(DOMAINS * ATOMS_DEV) % ATOMS_DEV == 0, NBR, counts)
    return counts.astype(jnp.int32)


def levels(rng, dims, cuts, least, high):
    def one(axis_at, shards_of):
        heights = jax.random.uniform(jax.random.fold_in(jax.random.fold_in(rng, 6), axis_at), (shards_of,), jnp.float32, least / len(cuts), high / len(cuts))
        return jnp.repeat(jnp.exp(heights), dims[axis_at] // shards_of).reshape((-1,) + (1,) * (len(dims) - axis_at - 1))

    factor_of = one(*cuts[0])
    for cut in cuts[1:]:
        factor_of = factor_of * one(*cut)
    return factor_of


def bell_draw(key, dims, deviation, bound, cuts=(), kind=jnp.bfloat16):
    drawn = jax.random.normal(key, dims, jnp.float32) * deviation
    if len(cuts) > 0:
        drawn = levels(key, dims, cuts, -0.22, 0.18) * drawn
    return jnp.clip(drawn, min=-bound, max=bound).astype(kind)


def setup_inputs(seed: int = 0) -> dict:
    keys = jax.random.split(jax.random.key(seed), 14)
    positions = bell_draw(keys[0], (BEADS, 3, ATOMS), 1.0, 6.0, ((0, 2), (2, 16)), jnp.float32)
    momenta = bell_draw(keys[1], (BEADS, 3, ATOMS), 1.0, 6.0, ((0, 2), (2, 16)), jnp.float32)
    neighbours = draw_neighbours(jax.random.fold_in(keys[13], 71), 0)
    nbr_count = draw_nbr_count(jax.random.fold_in(keys[13], 71), 0)
    send_rows = draw_send_rows(jax.random.fold_in(keys[13], 71), 0)
    embed_first = bell_draw(keys[5], (2, EMB), 1.5, 6.0, (), jnp.float32)
    embed_weight = bell_draw(keys[6], (EMB, EMB), EMB ** -0.5, 0.5)
    embed_bias = bell_draw(keys[7], (EMB,), 0.5, 3.0, (), jnp.float32)
    fit_weight = bell_draw(keys[8], (EMB * AXIS, FIT), (EMB * AXIS) ** -0.5, 0.125)
    fit_bias = bell_draw(keys[9], (FIT,), 0.5, 3.0, (), jnp.float32)
    fit_weight2 = bell_draw(keys[10], (FIT, FIT), FIT ** -0.5, 0.375)
    fit_bias2 = bell_draw(keys[11], (FIT,), 0.5, 3.0, (), jnp.float32)
    fit_out = bell_draw(keys[12], (FIT,), FIT ** -0.5, 0.375, (), jnp.float32)
    return dict(positions=positions, momenta=momenta, neighbours=neighbours, nbr_count=nbr_count, send_rows=send_rows, embed_first=embed_first, embed_weight=embed_weight, embed_bias=embed_bias, fit_weight=fit_weight, fit_bias=fit_bias, fit_weight2=fit_weight2, fit_bias2=fit_bias2, fit_out=fit_out)


cycle_freq = 0.5
time_step = 1.0
soften = 0.25
force_gain = 64.0

def mode_maps(beads):
    column = np.arange(beads)[None, :]
    bead_row = np.arange(beads)[:, None]
    phases = 2.0 * np.pi * bead_row * column / beads
    mode_basis = np.where(column == 0, 1.0 / np.sqrt(beads), np.where(2 * column < beads, np.sqrt(2.0 / beads) * np.cos(phases), np.where(2 * column == beads, np.cos(phases) / np.sqrt(beads), np.sqrt(2.0 / beads) * np.sin(phases))))
    frequency = 2.0 * cycle_freq * np.sin(np.pi * np.arange(beads) / beads)
    angles = frequency * time_step
    safe_freq = np.where(frequency > 0, frequency, 1.0)
    cosine = np.cos(angles)
    drift = np.where(frequency > 0, np.sin(angles) / safe_freq, time_step)
    pull = -frequency * np.sin(angles)
    keep_map = mode_basis * cosine[None, :] @ mode_basis.T
    drift_map = mode_basis * drift[None, :] @ mode_basis.T
    pull_map = mode_basis * pull[None, :] @ mode_basis.T
    return (jnp.asarray(keep_map, jnp.float32), jnp.asarray(drift_map, jnp.float32), jnp.asarray(pull_map, jnp.float32))

def site_energy(coord_table, neighbours, nbr_count, embed_first, embed_weight, embed_bias, fit_weight, fit_bias, fit_weight2, fit_bias2, fit_out):
    owned = neighbours.shape[0]
    listed = neighbours.shape[1]
    centre = coord_table[:, :owned]
    nearby = jnp.take(coord_table, neighbours, axis=1)
    offset_vec = nearby - centre[:, :, None]
    inverse = lax.rsqrt(lax.optimization_barrier(jnp.sum(offset_vec * offset_vec, axis=0)) + soften)
    active = (jnp.arange(listed)[None, :] < nbr_count[:, None]).astype(jnp.float32)
    smooth = inverse * active
    radial = jnp.concatenate([smooth[None], smooth[None] * inverse[None] * offset_vec], axis=0)
    embed_one = jnp.tanh(smooth[:, :, None] * embed_first[0] + embed_first[1])
    embed_low = embed_one.astype(jnp.bfloat16).reshape(owned * listed, -1)
    product = jnp.dot(embed_low, embed_weight, preferred_element_type=jnp.float32)
    second = embed_one + jnp.tanh(product.reshape(owned, listed, -1) + embed_bias)
    moment = jnp.einsum('xan,ane->axe', radial, second, precision=lax.Precision.HIGHEST) / listed
    descriptor = jnp.einsum('axe,axf->aef', moment, moment[:, :, :AXIS], precision=lax.Precision.HIGHEST).reshape(owned, -1)
    hidden = jnp.tanh(jnp.dot(descriptor.astype(jnp.bfloat16), fit_weight, preferred_element_type=jnp.float32) + fit_bias)
    hidden_two = hidden + jnp.tanh(jnp.dot(hidden.astype(jnp.bfloat16), fit_weight2, preferred_element_type=jnp.float32) + fit_bias2)
    return jnp.sum(hidden_two * fit_out)

def bead_forces(coord_table, neighbours, nbr_count, *params):
    return -jax.grad(site_energy)(coord_table, neighbours, nbr_count, *params)

def shift_domains(array, amount):
    filler = jnp.zeros((abs(amount),) + array.shape[1:], array.dtype)
    if amount > 0:
        return jnp.concatenate([filler, array[:-amount]], axis=0)
    return jnp.concatenate([array[-amount:], filler], axis=0)

def take_columns(flat_coords, picked):
    return jnp.take(flat_coords, picked, axis=1)

def add_columns(totals, picked, values):
    return totals.at[:, picked.reshape(-1)].add(values.reshape(values.shape[0], -1))

def reference(positions, momenta, neighbours, nbr_count, send_rows, embed_first, embed_weight, embed_bias, fit_weight, fit_bias, fit_weight2, fit_bias2, fit_out):
    params = (embed_first, embed_weight, embed_bias, fit_weight, fit_bias, fit_weight2, fit_bias2, fit_out)
    strides = list(range(-REACH, 0)) + list(range(1, REACH + 1))
    local_rows = positions.reshape(BEADS * 3, DOMAINS, ATOMS_DEV).transpose(1, 0, 2)
    filled = (send_rows >= 0).astype(jnp.float32)
    picked = jnp.maximum(send_rows, 0)
    packets = jax.vmap(take_columns)(local_rows, picked) * filled[:, None]
    ghost_list = []
    for column, stride in enumerate(strides):
        ghost_list.append(shift_domains(packets[:, :, column], stride))
    ghosts = jnp.stack(ghost_list, axis=2)
    coord_table = jnp.concatenate([local_rows, ghosts.reshape(DOMAINS, BEADS * 3, -1)], axis=2)
    coord_table = coord_table.reshape(DOMAINS, BEADS, 3, -1)

    def domain_forces(inputs):
        tables, nbr_here, count_here = inputs

        def per_bead(single):
            return bead_forces(single, nbr_here, count_here, *params)
        return lax.map(per_bead, tables)
    forces = lax.map(domain_forces, (coord_table, neighbours.reshape(DOMAINS, ATOMS_DEV, -1), nbr_count.reshape(DOMAINS, ATOMS_DEV)))
    forces = forces.reshape(DOMAINS, BEADS * 3, -1)
    own_force = forces[:, :, :ATOMS_DEV]
    ghost_force = forces[:, :, ATOMS_DEV:].reshape(DOMAINS, BEADS * 3, 2 * REACH, GSLOT)
    returned = []
    for column, stride in enumerate(strides):
        returned.append(shift_domains(ghost_force[:, :, column], -stride))
    returned = jnp.stack(returned, axis=2) * filled[:, None]
    own_force = jax.vmap(add_columns)(own_force, picked, returned)
    force_field = own_force.transpose(1, 0, 2).reshape(BEADS, 3, ATOMS)
    kicked = momenta + time_step * force_gain * force_field
    keep_map, drift_map, pull_map = mode_maps(BEADS)
    flat_q = positions.reshape(BEADS, -1)
    flat_p = kicked.reshape(BEADS, -1)
    highest = lax.Precision.HIGHEST
    new_positions = jnp.dot(keep_map, flat_q, precision=highest) + jnp.dot(drift_map, flat_p, precision=highest)
    new_momenta = jnp.dot(pull_map, flat_q, precision=highest) + jnp.dot(keep_map, flat_p, precision=highest)
    return (new_positions.reshape(positions.shape), new_momenta.reshape(positions.shape))
```

```python
import functools

import jax
import jax.numpy as jnp
import numpy as np
from jax import lax
from jax.experimental import pallas as pl
from jax.experimental.pallas import tpu as pltpu
from jax.sharding import PartitionSpec as P

AXIS = 16
LANES = 128
GROUP = 8

cycle_freq = 0.5
time_step = 1.0
soften = 0.25
force_gain = 64.0

f32 = jnp.float32
bf16 = jnp.bfloat16


def passed_along(value, axis, steps):
    count = lax.axis_size(axis)
    first, last = (max(0, -steps), min(count, count - steps))
    return lax.ppermute(value, axis, [(source, source + steps) for source in range(first, last)])


def mode_maps(beads):
    column = np.arange(beads)[None, :]
    bead_row = np.arange(beads)[:, None]
    phases = 2.0 * np.pi * bead_row * column / beads
    mode_basis = np.where(
        column == 0,
        1.0 / np.sqrt(beads),
        np.where(
            2 * column < beads,
            np.sqrt(2.0 / beads) * np.cos(phases),
            np.where(
                2 * column == beads,
                np.cos(phases) / np.sqrt(beads),
                np.sqrt(2.0 / beads) * np.sin(phases),
            ),
        ),
    )
    frequency = 2.0 * cycle_freq * np.sin(np.pi * np.arange(beads) / beads)
    angles = frequency * time_step
    safe_freq = np.where(frequency > 0, frequency, 1.0)
    cosine = np.cos(angles)
    drift = np.where(frequency > 0, np.sin(angles) / safe_freq, time_step)
    pull = -frequency * np.sin(angles)
    keep_map = mode_basis * cosine[None, :] @ mode_basis.T
    drift_map = mode_basis * drift[None, :] @ mode_basis.T
    pull_map = mode_basis * pull[None, :] @ mode_basis.T
    return keep_map, drift_map, pull_map


def propagation_table(groups, bead_dev):
    keep, drift, pull = mode_maps(groups * bead_dev)
    table = np.zeros((groups, groups, 2, bead_dev, 3, 2, 3, bead_dev))
    for source in range(groups):
        cols = slice(source * bead_dev, (source + 1) * bead_dev)
        for target in range(groups):
            rows = slice(target * bead_dev, (target + 1) * bead_dev)
            for c in range(3):
                table[source, target, 0, :, c, 0, c, :] = keep[rows, cols]
                table[source, target, 0, :, c, 1, c, :] = drift[rows, cols]
                table[source, target, 1, :, c, 0, c, :] = pull[rows, cols]
                table[source, target, 1, :, c, 1, c, :] = keep[rows, cols]
    if groups == 2:
        table[1] = table[1, ::-1].copy()
    return table.reshape(groups, groups * 6 * bead_dev, 6 * bead_dev).astype(np.float32)


def lane_take(values, picked):
    numbers = lax.GatherDimensionNumbers(
        offset_dims=(),
        collapsed_slice_dims=(1,),
        start_index_map=(1,),
        operand_batching_dims=(0,),
        start_indices_batching_dims=(0,),
    )
    return lax.gather(
        values,
        picked[..., None],
        numbers,
        (1, 1),
        mode=lax.GatherScatterMode.PROMISE_IN_BOUNDS,
    )


def dot(a, b):
    return jnp.dot(a, b, preferred_element_type=f32)


def dot_nt(a, b):
    return lax.dot_general(a, b, (((1,), (1,)), ((), ())), preferred_element_type=f32)


def packet_kernel(pos, send, own, *outs_and_scratch):
    outs, table = outs_and_scratch[:-1], outs_and_scratch[-1]
    beads, comps, atoms = pos.shape
    table[...] = jnp.zeros_like(table)
    for b in range(beads):
        for c in range(comps):
            row = c * beads + b
            table[row : row + 1, 0:atoms] = pos[b, c : c + 1, :]
    own[...] = table[0 : beads * comps, 0:atoms]
    for j, out in enumerate(outs):
        picked = send[0, j : j + 1, :]
        for first in range(0, beads * comps, 8):
            rows = min(8, beads * comps - first)
            wide = jnp.concatenate([picked, jnp.full((1, LANES - atoms), -1, jnp.int32)], axis=1)
            wide = jnp.broadcast_to(wide, (8, LANES))
            got = lane_take(table[first : first + 8, :], jnp.maximum(wide, 0))
            got = jnp.where(wide >= 0, got, 0.0)
            out[first : first + rows, :] = got[0:rows, 0:atoms]


def column_of(row, rows):
    wide = jnp.broadcast_to(row, (LANES, rows))
    return jnp.transpose(wide)


def wide_columns(column, width):
    return jnp.concatenate([column] * (width // LANES), axis=1)


def force_kernel(
    own, g0, g1, g2, g3, idx, cnt, first, w_embed_t, e_bias,
    fit_w, fit_wt, f_bias, fit_w2, fit_w2t, f_bias2, f_out,
    own_f, o0, o1, o2, o3,
    table, counts, columns, fit_columns, radial, inverse, offset, second, slope,
    moment, moment_t, desc, d_desc, d_moment_t, d_moment, pair_grad, totals, index,
):
    beads = 4
    comps = 3
    atoms = own.shape[1]
    blocks, width = idx.shape
    listed = width // GROUP
    emb = w_embed_t.shape[0]
    fit = f_bias.shape[1]
    fit_pad = fit_w.shape[1]
    sources = (own, g0, g1, g2, g3)

    table[...] = jnp.zeros_like(table)
    for j, source in enumerate(sources):
        for c in range(comps):
            table[j, c, 0:beads, 0:atoms] = source[c * beads : (c + 1) * beads, :]
    counts[...] = jnp.zeros_like(counts)
    counts[:, 0:atoms] = jnp.broadcast_to(cnt[...], (8, atoms))
    columns[0] = column_of(first[0:1, :], emb)
    columns[1] = column_of(first[1:2, :], emb)
    columns[2] = column_of(e_bias[...], emb)
    pad = jnp.zeros((1, fit_pad - fit), f32)
    for at, vector in enumerate((f_bias, f_bias2, f_out)):
        fit_columns[at] = column_of(jnp.concatenate([vector[...], pad], axis=1), fit_pad)
    pair_grad[...] = jnp.zeros_like(pair_grad)
    totals[...] = jnp.zeros_like(totals)
    for i in range(blocks):
        index[i] = jnp.broadcast_to(idx[i : i + 1, :], (8, width))

    lane = lax.broadcasted_iota(jnp.int32, (8, LANES), 1)

    def pairs(i, carry):
        for part in range(width // LANES):
            cols = slice(part * LANES, (part + 1) * LANES)
            ix = index[i, :, cols]
            atom = GROUP * i + part * (LANES // listed) + lane // listed
            entry = lane % listed
            domain = (ix >= atoms).astype(jnp.int32)
            for j in range(2, len(sources)):
                domain += (ix >= j * atoms).astype(jnp.int32)
            local = ix - atoms * domain
            active = entry < lane_take(counts[...], atom)
            offs = []
            for c in range(comps):
                near = lane_take(table[0, c], local)
                for j in range(1, len(sources)):
                    near = jnp.where(domain == j, lane_take(table[j, c], local), near)
                offs.append(near - lane_take(table[0, c], atom))
            square = offs[0] * offs[0] + offs[1] * offs[1] + offs[2] * offs[2]
            inv = lax.rsqrt(square + soften)
            smooth = jnp.where(active, inv, 0.0)
            scaled = smooth * inv
            inverse[i, :, cols] = inv
            radial[0, i, :, cols] = smooth
            for c in range(comps):
                offset[c, i, :, cols] = offs[c]
                radial[c + 1, i, :, cols] = scaled * offs[c]
        return carry

    lax.fori_loop(0, blocks, pairs, 0)

    segment = (
        lax.broadcasted_iota(jnp.int32, (GROUP, width), 1) // listed
        == lax.broadcasted_iota(jnp.int32, (GROUP, width), 0)
    )

    def embed(i, carry):
        for b in range(beads):
            w_first = wide_columns(columns[0], width)
            smooth = radial[0, i, b : b + 1, :]
            one = jnp.tanh(smooth * w_first + wide_columns(columns[1], width))
            one_slope = (1.0 - one * one) * w_first
            low = jnp.concatenate([one.astype(bf16), one_slope.astype(bf16)], axis=1)
            product = dot(w_embed_t[...], low)
            two = jnp.tanh(product[:, 0:width] + wide_columns(columns[2], width))
            total = (one + two).astype(bf16)
            second[b * blocks + i] = total
            slope[b * blocks + i] = (one_slope + (1.0 - two * two) * product[:, width:]).astype(bf16)
            spread = jnp.concatenate(
                [jnp.where(segment, radial[x, i, b : b + 1, :], 0.0) for x in range(4)], axis=0
            )
            part = dot_nt(spread.astype(bf16), total) * (1.0 / listed)
            start = pl.multiple_of(b * atoms + GROUP * i, GROUP)
            for x in range(4):
                moment[x, pl.ds(start, GROUP), :] = part[x * GROUP : (x + 1) * GROUP, :]
        return carry

    lax.fori_loop(0, blocks, embed, 0)

    for x in range(4):
        moment_t[x] = jnp.transpose(moment[x])
    for f in range(AXIS):
        value = moment_t[0] * moment_t[0, f : f + 1, :]
        for x in range(1, 4):
            value += moment_t[x] * moment_t[x, f : f + 1, :]
        desc[f * emb : (f + 1) * emb, :] = value.astype(bf16)
    many = beads * atoms
    bias, bias2, out_col = (wide_columns(fit_columns[at], many) for at in range(3))
    hidden = jnp.tanh(dot(fit_wt[...], desc[...]) + bias)
    more = jnp.tanh(dot(fit_w2t[...], hidden.astype(bf16)) + bias2)
    d_more = out_col * (1.0 - more * more)
    d_hidden = out_col + dot(fit_w2[...], d_more.astype(bf16))
    d_pre = (d_hidden * (1.0 - hidden * hidden)).astype(bf16)
    d_desc[...] = dot(fit_w[...], d_pre)

    def left(e, carry):
        rows = pl.ds(pl.multiple_of(e * 8, 8), 8)
        sums = [None] * 4
        for f in range(AXIS):
            grad = d_desc[pl.ds(pl.multiple_of(f * emb + e * 8, 8), 8), :]
            for x in range(4):
                term = grad * moment_t[x, f : f + 1, :]
                sums[x] = term if f == 0 else sums[x] + term
        for x in range(4):
            d_moment_t[x, rows, :] = sums[x]
        return carry

    lax.fori_loop(0, emb // 8, left, 0)
    for f in range(AXIS):
        for x in range(4):
            terms = jnp.sum(d_desc[f * emb : (f + 1) * emb, :] * moment_t[x], axis=0, keepdims=True)
            d_moment_t[x, f : f + 1, :] += terms
    for x in range(4):
        d_moment[x] = jnp.transpose(d_moment_t[x]) * (1.0 / listed)

    row_of = lax.broadcasted_iota(jnp.int32, (atoms, width), 0)
    lane_of = lax.broadcasted_iota(jnp.int32, (atoms, width), 1)

    def backward(i, carry):
        for b in range(beads):
            start = pl.multiple_of(b * atoms + GROUP * i, GROUP)
            left_side = jnp.concatenate(
                [d_moment[x, pl.ds(start, GROUP), :] for x in range(4)], axis=0
            ).astype(bf16)
            by_second = dot(left_side, second[b * blocks + i])
            by_slope = dot(left_side, slope[b * blocks + i])
            along = None
            for x in range(4):
                rows = slice(x * GROUP, (x + 1) * GROUP)
                pair_grad[x, b : b + 1, :] = jnp.sum(
                    jnp.where(segment, by_second[rows, :], 0.0), axis=0, keepdims=True
                )
                term = by_slope[rows, :] * radial[x, i, b : b + 1, :]
                along = term if along is None else along + term
            pair_grad[4, b : b + 1, :] = jnp.sum(
                jnp.where(segment, along, 0.0), axis=0, keepdims=True
            )
        inv = inverse[i]
        smooth = radial[0, i]
        offs = [offset[c, i] for c in range(comps)]
        along = pair_grad[1] * offs[0] + pair_grad[2] * offs[1] + pair_grad[3] * offs[2]
        live = jnp.where(smooth > 0.0, 1.0, 0.0)
        d_inv = live * (pair_grad[0] + pair_grad[4]) + 2.0 * smooth * along
        pull = d_inv * inv * inv * inv
        scaled = smooth * inv
        grads = [pair_grad[c + 1] * scaled - pull * offs[c] for c in range(comps)]
        high = [g.astype(bf16) for g in grads]
        low = [(g - h.astype(f32)) for g, h in zip(grads, high)]
        sides = jnp.concatenate(
            [h.astype(f32) for h in high] + low, axis=0
        ).astype(bf16)
        ix = index[i, 0:1, :]
        for j in range(len(sources)):
            hot = jnp.where(row_of == ix - j * atoms, 1.0, 0.0)
            if j == 0:
                hot = hot - jnp.where(row_of == GROUP * i + lane_of // listed, 1.0, 0.0)
            totals[j * LANES : j * LANES + atoms, 0 : 6 * 8] += dot_nt(hot.astype(bf16), sides)
        return carry

    lax.fori_loop(0, blocks, backward, 0)

    for j, out in enumerate((own_f, o0, o1, o2, o3)):
        turned = jnp.transpose(totals[j * LANES : (j + 1) * LANES, :])
        whole = turned[0:24, :] + turned[24:48, :]
        for c in range(comps):
            out[c * beads : (c + 1) * beads, :] = -whole[c * 8 : c * 8 + beads, 0:atoms]


def finish_kernel(pos, mom, own_f, r0, r1, r2, r3, send, maps, out, stacked):
    beads, comps, atoms = pos.shape
    rows = beads * comps
    force = own_f[...]
    row_of = lax.broadcasted_iota(jnp.int32, (atoms, send.shape[2]), 0)
    for j, back in enumerate((r0, r1, r2, r3)):
        hot = jnp.where(row_of == send[0, j : j + 1, :], 1.0, 0.0).astype(bf16)
        value = back[...]
        high = value.astype(bf16)
        rest = value - high.astype(f32)
        low = rest.astype(bf16)
        force += dot_nt(high, hot) + dot_nt(low, hot)
    stacked[rows:, :] = force * (time_step * force_gain)
    for b in range(beads):
        for c in range(comps):
            at = c * beads + b
            stacked[at : at + 1, :] = pos[b, c : c + 1, :]
            stacked[rows + at : rows + at + 1, :] += mom[b, c : c + 1, :]
    out[...] = jnp.dot(
        maps[lax.axis_index("bead")],
        stacked[...],
        precision=lax.Precision.HIGHEST,
        preferred_element_type=f32,
    )


def on_device(
    positions, momenta, neighbours, nbr_count, send_rows, embed_first, embed_weight,
    embed_bias, fit_weight, fit_bias, fit_weight2, fit_bias2, fit_out,
):
    bead_dev, comps, atoms = positions.shape
    listed = neighbours.shape[1]
    fit = fit_weight.shape[1]
    emb = embed_weight.shape[0]
    fit_pad = -(-fit // LANES) * LANES
    rows = bead_dev * comps
    blocks = atoms // GROUP
    width = GROUP * listed
    many = bead_dev * atoms
    piece = jax.ShapeDtypeStruct((rows, atoms), f32)
    strides = (-2, -1, 1, 2)

    own, *packets = pl.pallas_call(
        packet_kernel,
        out_shape=[piece] * 5,
        scratch_shapes=[pltpu.VMEM((16, LANES), f32)],
        name="packets",
    )(positions, send_rows)
    ghosts = [passed_along(packet, "space", stride) for packet, stride in zip(packets, strides)]

    by_axis = fit_weight.reshape(emb, AXIS, fit).transpose(1, 0, 2).reshape(emb * AXIS, fit)
    fit_w = jnp.pad(by_axis, ((0, 0), (0, fit_pad - fit)))
    fit_wt = fit_w.T
    fit_w2 = jnp.pad(fit_weight2, ((0, fit_pad - fit), (0, fit_pad - fit)))
    own_f, *ghost_f = pl.pallas_call(
        force_kernel,
        out_shape=[piece] * 5,
        scratch_shapes=[
            pltpu.VMEM((5, comps, 8, LANES), f32),
            pltpu.VMEM((8, LANES), jnp.int32),
            pltpu.VMEM((3, emb, LANES), f32),
            pltpu.VMEM((3, fit_pad, LANES), f32),
            pltpu.VMEM((4, blocks, 8, width), f32),
            pltpu.VMEM((blocks, 8, width), f32),
            pltpu.VMEM((comps, blocks, 8, width), f32),
            pltpu.VMEM((bead_dev * blocks, emb, width), bf16),
            pltpu.VMEM((bead_dev * blocks, emb, width), bf16),
            pltpu.VMEM((4, many, emb), f32),
            pltpu.VMEM((4, emb, many), f32),
            pltpu.VMEM((emb * AXIS, many), bf16),
            pltpu.VMEM((emb * AXIS, many), f32),
            pltpu.VMEM((4, emb, many), f32),
            pltpu.VMEM((4, many, emb), f32),
            pltpu.VMEM((5, 8, width), f32),
            pltpu.VMEM((5 * LANES, LANES), f32),
            pltpu.VMEM((blocks, 8, width), jnp.int32),
        ],
        compiler_params=pltpu.CompilerParams(vmem_limit_bytes=50 * 1024 * 1024),
        name="forces",
    )(
        own, *ghosts, neighbours.reshape(blocks, width), nbr_count.reshape(1, atoms),
        embed_first, embed_weight.T, embed_bias.reshape(1, emb),
        fit_w, fit_wt, fit_bias.reshape(1, fit), fit_w2, fit_w2.T,
        fit_bias2.reshape(1, fit), fit_out.reshape(1, fit),
    )
    returned = [passed_along(part, "space", -stride) for part, stride in zip(ghost_f, strides)]

    groups = lax.axis_size("bead")
    maps = jnp.asarray(propagation_table(groups, bead_dev))
    shares = pl.pallas_call(
        finish_kernel,
        out_shape=jax.ShapeDtypeStruct((groups * 2 * rows, atoms), f32),
        scratch_shapes=[pltpu.VMEM((2 * rows, atoms), f32)],
        name="propagate",
    )(positions, momenta, own_f, *returned, send_rows, maps)
    if groups == 2:
        other = lax.ppermute(shares[2 * rows :], "bead", [(0, 1), (1, 0)])
        result = shares[: 2 * rows] + other
    else:
        parts = lax.all_to_all(
            shares.reshape(groups, 2 * rows, atoms), "bead", split_axis=0, concat_axis=0, tiled=True
        )
        result = parts.sum(axis=0)
    return (result[:rows].reshape(positions.shape), result[rows:].reshape(positions.shape))


def solution(mesh):
    in_specs = (
        P("bead", None, "space"),
        P("bead", None, "space"),
        P("space", None),
        P("space"),
        P("space", None, None),
    ) + (P(),) * 8
    out_specs = (P("bead", None, "space"), P("bead", None, "space"))
    return jax.shard_map(
        on_device, mesh=mesh, in_specs=in_specs, out_specs=out_specs, check_vma=False
    )
```

```python
import functools

import jax
import jax.numpy as jnp
import numpy as np
from jax import lax
from jax.experimental import pallas as pl
from jax.experimental.pallas import tpu as pltpu
from jax.sharding import PartitionSpec as P

AXIS = 16
LANES = 128
GROUP = 8

cycle_freq = 0.5
time_step = 1.0
soften = 0.25
force_gain = 64.0

f32 = jnp.float32
bf16 = jnp.bfloat16


def passed_along(value, axis, steps):
    count = lax.axis_size(axis)
    first, last = (max(0, -steps), min(count, count - steps))
    return lax.ppermute(value, axis, [(source, source + steps) for source in range(first, last)])


def mode_maps(beads):
    column = np.arange(beads)[None, :]
    bead_row = np.arange(beads)[:, None]
    phases = 2.0 * np.pi * bead_row * column / beads
    mode_basis = np.where(
        column == 0,
        1.0 / np.sqrt(beads),
        np.where(
            2 * column < beads,
            np.sqrt(2.0 / beads) * np.cos(phases),
            np.where(
                2 * column == beads,
                np.cos(phases) / np.sqrt(beads),
                np.sqrt(2.0 / beads) * np.sin(phases),
            ),
        ),
    )
    frequency = 2.0 * cycle_freq * np.sin(np.pi * np.arange(beads) / beads)
    angles = frequency * time_step
    safe_freq = np.where(frequency > 0, frequency, 1.0)
    cosine = np.cos(angles)
    drift = np.where(frequency > 0, np.sin(angles) / safe_freq, time_step)
    pull = -frequency * np.sin(angles)
    keep_map = mode_basis * cosine[None, :] @ mode_basis.T
    drift_map = mode_basis * drift[None, :] @ mode_basis.T
    pull_map = mode_basis * pull[None, :] @ mode_basis.T
    return keep_map, drift_map, pull_map


def propagation_table(groups, bead_dev):
    keep, drift, pull = mode_maps(groups * bead_dev)
    table = np.zeros((groups, groups, 2, bead_dev, 3, 2, 3, bead_dev))
    for source in range(groups):
        cols = slice(source * bead_dev, (source + 1) * bead_dev)
        for target in range(groups):
            rows = slice(target * bead_dev, (target + 1) * bead_dev)
            for c in range(3):
                table[source, target, 0, :, c, 0, c, :] = keep[rows, cols]
                table[source, target, 0, :, c, 1, c, :] = drift[rows, cols]
                table[source, target, 1, :, c, 0, c, :] = pull[rows, cols]
                table[source, target, 1, :, c, 1, c, :] = keep[rows, cols]
    if groups == 2:
        table[1] = table[1, ::-1].copy()
    table = table.reshape(groups, groups * 6 * bead_dev, 6 * bead_dev)
    return np.pad(table, ((0, 0), (0, 0), (0, LANES - table.shape[2]))).astype(np.float32)


def lane_take(values, picked):
    numbers = lax.GatherDimensionNumbers(
        offset_dims=(),
        collapsed_slice_dims=(1,),
        start_index_map=(1,),
        operand_batching_dims=(0,),
        start_indices_batching_dims=(0,),
    )
    return lax.gather(
        values,
        picked[..., None],
        numbers,
        (1, 1),
        mode=lax.GatherScatterMode.PROMISE_IN_BOUNDS,
    )


def dot(a, b):
    return jnp.dot(a, b, preferred_element_type=f32)


def dot_nt(a, b):
    return lax.dot_general(a, b, (((1,), (1,)), ((), ())), preferred_element_type=f32)


def column_of(row, rows):
    wide = jnp.broadcast_to(row, (LANES, rows))
    return jnp.transpose(wide)


def wide_columns(column, width):
    return jnp.concatenate([column] * (width // LANES), axis=1)


def split_dot(a, b):
    high = b.astype(bf16)
    return dot(a, high) + dot(a, (b - high.astype(f32)).astype(bf16))


def prepare_kernel(first, w_embed, e_bias, fit_w, f_bias, fit_w2, f_bias2, f_out,
                   w_embed_t, fit_rows, fit_cols, fit_w2_pad, fit_w2t, columns, fit_columns):
    emb = w_embed.shape[0]
    fit = fit_w.shape[1]
    fit_pad = fit_rows.shape[1]

    def unit(n):
        same = lax.broadcasted_iota(jnp.int32, (n, n), 0) == lax.broadcasted_iota(jnp.int32, (n, n), 1)
        return jnp.where(same, 1.0, 0.0).astype(bf16)

    w_embed_t[...] = dot_nt(unit(emb), w_embed[...]).astype(bf16)
    fit_w2_pad[...] = jnp.zeros_like(fit_w2_pad)
    fit_w2_pad[0:fit, 0:fit] = fit_w2[...]
    fit_w2t[...] = dot_nt(unit(fit_pad), fit_w2_pad[...]).astype(bf16)
    row = lax.broadcasted_iota(jnp.int32, (LANES, LANES), 0)
    source = AXIS * (row % 8) + row // 8
    order = jnp.where(lax.broadcasted_iota(jnp.int32, (LANES, LANES), 1) == source, 1.0, 0.0).astype(bf16)
    fit_rows[:, LANES:] = jnp.zeros((fit_rows.shape[0], fit_pad - LANES), bf16)
    for chunk in range(fit_w.shape[0] // LANES):
        part = slice(chunk * LANES, (chunk + 1) * LANES)
        fit_rows[part, 0:fit] = dot(order, fit_w[part, :]).astype(bf16)
        fit_cols[:, part] = dot_nt(unit(fit_pad), fit_rows[part, :]).astype(bf16)
    columns[0] = column_of(first[0:1, :], emb)
    columns[1] = column_of(first[1:2, :], emb)
    columns[2] = column_of(e_bias[...], emb)
    for at, vector in enumerate((f_bias, f_bias2, f_out)):
        pad = jnp.zeros((1, fit_pad - fit), f32)
        fit_columns[at] = column_of(jnp.concatenate([vector[...], pad], axis=1), fit_pad)


def force_kernel(
    own, core, link, far, idx, cnt, w_embed_t, fit_w, fit_wt, columns, fit_columns, fit_w2, fit_w2t,
    own_f, near_f, link_f,
    table, counts, sent, radial, inverse, offset, second, slope,
    moment, moment_t, desc, d_desc, d_moment_t, d_moment, pair_grad, totals, index,
    rows_here, cols_here, loaded,
):
    beads = 4
    comps = 3
    atoms = own.shape[1]
    blocks, width = idx.shape
    listed = width // GROUP
    emb = w_embed_t.shape[0]
    fit = fit_w2.shape[0]
    rows = beads * comps
    loads = [
        pltpu.make_async_copy(fit_wt, cols_here, loaded.at[0]),
        pltpu.make_async_copy(fit_w, rows_here, loaded.at[1]),
    ]
    for load in loads:
        load.start()

    odd = lax.rem(lax.axis_index("space"), 2) == 1
    block_of = ((2, 1), (1, 2), (0, 3), (3, 0))
    table[...] = jnp.zeros_like(table)
    sent[...] = jnp.zeros_like(sent)
    sources = ((own, 0), (core, 0), (link, 0), (link, own.shape[0]), (far, 0))
    for role, (source, at) in enumerate(sources):
        for c in range(comps):
            table[role, c, 0:beads, 0:atoms] = source[at + c * beads : at + (c + 1) * beads, :]
        if role > 0:
            if_odd, if_even = (
                source[at + rows + j : at + rows + j + 1, :] for j in block_of[role - 1]
            )
            row = jnp.maximum(jnp.where(odd, if_odd, if_even), 0.0).astype(jnp.int32)
            sent[role - 1, :, 0:atoms] = jnp.broadcast_to(row, (8, atoms))
    role_of = [
        jnp.where(odd, 1 + [pair[0] for pair in block_of].index(j), 1 + [pair[1] for pair in block_of].index(j))
        for j in range(4)
    ]
    counts[...] = jnp.zeros_like(counts)
    counts[:, 0:atoms] = jnp.broadcast_to(cnt[...], (8, atoms))
    pair_grad[...] = jnp.zeros_like(pair_grad)
    totals[...] = jnp.zeros_like(totals)
    for i in range(blocks):
        index[i] = jnp.broadcast_to(idx[i : i + 1, :], (8, width))

    lane = lax.broadcasted_iota(jnp.int32, (8, LANES), 1)

    def pairs(i, carry):
        for part in range(width // LANES):
            cols = slice(part * LANES, (part + 1) * LANES)
            ix = index[i, :, cols]
            atom = GROUP * i + part * (LANES // listed) + lane // listed
            entry = lane % listed
            role = jnp.where(ix >= atoms, role_of[0], 0)
            block = jnp.where(ix >= atoms, 1, 0)
            for j in range(1, 4):
                role = jnp.where(ix >= (j + 1) * atoms, role_of[j], role)
                block = jnp.where(ix >= (j + 1) * atoms, j + 1, block)
            slot = ix - atoms * block
            local = slot
            for r in range(1, 5):
                local = jnp.where(role == r, lane_take(sent[r - 1], slot), local)
            index[i, :, cols] = local + role * LANES
            active = entry < lane_take(counts[...], atom)
            offs = []
            for c in range(comps):
                near = lane_take(table[0, c], local)
                for j in range(1, len(sources)):
                    near = jnp.where(role == j, lane_take(table[j, c], local), near)
                offs.append(near - lane_take(table[0, c], atom))
            square = offs[0] * offs[0] + offs[1] * offs[1] + offs[2] * offs[2]
            inv = lax.rsqrt(square + soften)
            smooth = jnp.where(active, inv, 0.0)
            scaled = smooth * inv
            inverse[i, :, cols] = inv
            radial[0, i, :, cols] = smooth
            for c in range(comps):
                offset[c, i, :, cols] = offs[c]
                radial[c + 1, i, :, cols] = scaled * offs[c]
        return carry

    lax.fori_loop(0, blocks, pairs, 0)

    segment = (
        lax.broadcasted_iota(jnp.int32, (GROUP, width), 1) // listed
        == lax.broadcasted_iota(jnp.int32, (GROUP, width), 0)
    )

    def embed(i, carry):
        for b in range(beads):
            w_first = wide_columns(columns[0], width)
            smooth = radial[0, i, b : b + 1, :]
            one = jnp.tanh(smooth * w_first + wide_columns(columns[1], width))
            one_slope = (1.0 - one * one) * w_first
            low = jnp.concatenate([one.astype(bf16), one_slope.astype(bf16)], axis=1)
            product = dot(w_embed_t[...], low)
            two = jnp.tanh(product[:, 0:width] + wide_columns(columns[2], width))
            both = one + two
            total = both.astype(bf16)
            second[b * blocks + i] = total
            slope[b * blocks + i] = (one_slope + (1.0 - two * two) * product[:, width:]).astype(bf16)
            spread = jnp.concatenate(
                [jnp.where(segment, radial[x, i, b : b + 1, :], 0.0) for x in range(4)], axis=0
            )
            high = spread.astype(bf16)
            halves = jnp.concatenate([high, (spread - high.astype(f32)).astype(bf16)], axis=0)
            part = dot_nt(halves, total)
            rest = dot_nt(high, (both - total.astype(f32)).astype(bf16))
            part = (part[0 : 4 * GROUP, :] + part[4 * GROUP :, :] + rest) * (1.0 / listed)
            start = pl.multiple_of(b * atoms + GROUP * i, GROUP)
            for x in range(4):
                moment[x, pl.ds(start, GROUP), :] = part[x * GROUP : (x + 1) * GROUP, :]
        return carry

    lax.fori_loop(0, blocks, embed, 0)

    for x in range(4):
        moment_t[x] = jnp.transpose(moment[x])
    def describe(e, carry):
        mine = [moment_t[x, pl.ds(pl.multiple_of(e * 8, 8), 8), :] for x in range(4)]
        for f in range(0, AXIS, 2):
            values = []
            for g in (f, f + 1):
                value = mine[0] * moment_t[0, g : g + 1, :]
                for x in range(1, 4):
                    value += mine[x] * moment_t[x, g : g + 1, :]
                values.append(value)
            at = pl.ds(pl.multiple_of(e * 8 * AXIS + f * 8, 16), 16)
            desc[at, :] = jnp.concatenate(values, axis=0).astype(bf16)
        return carry

    lax.fori_loop(0, emb // 8, describe, 0)
    for load in loads:
        load.wait()
    many = beads * atoms
    bias, bias2, out_col = (wide_columns(fit_columns[at, 0:fit, :], many) for at in range(3))
    hidden = jnp.tanh(dot(cols_here[...], desc[...]) + bias)
    more = jnp.tanh(dot(fit_w2t[...], hidden.astype(bf16)) + bias2)
    d_more = out_col * (1.0 - more * more)
    d_hidden = out_col + split_dot(fit_w2[...], d_more).astype(bf16).astype(f32)
    d_pre = d_hidden * (1.0 - hidden * hidden)
    d_desc[...] = split_dot(rows_here[...], d_pre).astype(bf16).astype(f32)

    def left(e, carry):
        rows = pl.ds(pl.multiple_of(e * 8, 8), 8)
        sums = [None] * 4
        for f in range(AXIS):
            grad = d_desc[pl.ds(pl.multiple_of((e * AXIS + f) * 8, 8), 8), :]
            for x in range(4):
                term = grad * moment_t[x, f : f + 1, :]
                sums[x] = term if f == 0 else sums[x] + term
        for x in range(4):
            d_moment_t[x, rows, :] = sums[x]
        return carry

    lax.fori_loop(0, emb // 8, left, 0)
    for f in range(AXIS):
        terms = [None] * 4
        for e in range(emb // 8):
            grad = d_desc[(e * AXIS + f) * 8 : (e * AXIS + f + 1) * 8, :]
            for x in range(4):
                term = grad * moment_t[x, e * 8 : (e + 1) * 8, :]
                terms[x] = term if e == 0 else terms[x] + term
        for x in range(4):
            d_moment_t[x, f : f + 1, :] += jnp.sum(terms[x], axis=0, keepdims=True)
    for x in range(4):
        d_moment[x] = jnp.transpose(d_moment_t[x]) * (1.0 / listed)

    row_of = lax.broadcasted_iota(jnp.int32, (atoms, width), 0)
    lane_of = lax.broadcasted_iota(jnp.int32, (atoms, width), 1)

    def backward(i, carry):
        for b in range(beads):
            start = pl.multiple_of(b * atoms + GROUP * i, GROUP)
            left_side = jnp.concatenate(
                [d_moment[x, pl.ds(start, GROUP), :] for x in range(4)], axis=0
            )
            high = left_side.astype(bf16)
            halves = jnp.concatenate([high, (left_side - high.astype(f32)).astype(bf16)], axis=0)
            by_second = dot(halves, second[b * blocks + i])
            by_second = by_second[0 : 4 * GROUP, :] + by_second[4 * GROUP :, :]
            by_slope = dot(halves, slope[b * blocks + i])
            by_slope = by_slope[0 : 4 * GROUP, :] + by_slope[4 * GROUP :, :]
            along = None
            for x in range(4):
                rows = slice(x * GROUP, (x + 1) * GROUP)
                pair_grad[x, b : b + 1, :] = jnp.sum(
                    jnp.where(segment, by_second[rows, :], 0.0), axis=0, keepdims=True
                )
                term = by_slope[rows, :] * radial[x, i, b : b + 1, :]
                along = term if along is None else along + term
            pair_grad[4, b : b + 1, :] = jnp.sum(
                jnp.where(segment, along, 0.0), axis=0, keepdims=True
            )
        inv = inverse[i]
        smooth = radial[0, i]
        offs = [offset[c, i] for c in range(comps)]
        along = pair_grad[1] * offs[0] + pair_grad[2] * offs[1] + pair_grad[3] * offs[2]
        live = jnp.where(smooth > 0.0, 1.0, 0.0)
        d_inv = live * (pair_grad[0] + pair_grad[4]) + 2.0 * smooth * along
        pull = d_inv * inv * inv * inv
        scaled = smooth * inv
        grads = [pair_grad[c + 1] * scaled - pull * offs[c] for c in range(comps)]
        high = [g.astype(bf16) for g in grads]
        low = [(g - h.astype(f32)) for g, h in zip(grads, high)]
        sides = jnp.concatenate(
            [h.astype(f32) for h in high] + low, axis=0
        ).astype(bf16)
        ix = index[i, 0:1, :]
        for j in range(len(sources)):
            hot = jnp.where(row_of == ix - j * LANES, 1.0, 0.0)
            if j == 0:
                hot = hot - jnp.where(row_of == GROUP * i + lane_of // listed, 1.0, 0.0)
            totals[j * LANES : j * LANES + atoms, 0 : 6 * 8] += dot_nt(hot.astype(bf16), sides)
        return carry

    lax.fori_loop(0, blocks, backward, 0)

    targets = ((own_f, 0), (near_f, 0), (link_f, 0), (link_f, rows), (near_f, rows))
    for j, (out, at) in enumerate(targets):
        turned = jnp.transpose(totals[j * LANES : (j + 1) * LANES, :])
        whole = turned[0:24, :] + turned[24:48, :]
        for c in range(comps):
            out[at + c * beads : at + (c + 1) * beads, :] = -whole[c * 8 : c * 8 + beads, 0:atoms]


def finish_kernel(pos, mom, own_f, near, link, far, maps, *outs_and_scratch):
    outs, stacked = outs_and_scratch[:-1], outs_and_scratch[-1]
    beads, comps, atoms = pos.shape
    rows = beads * comps
    force = (own_f[...] + near[0:rows, :]) + (link[0:rows, :] + far[rows : 2 * rows, :])
    stacked[...] = jnp.zeros_like(stacked)
    stacked[rows : 2 * rows, 0:atoms] = force * (time_step * force_gain)
    for b in range(beads):
        for c in range(comps):
            at = c * beads + b
            stacked[at : at + 1, 0:atoms] = pos[b, c : c + 1, :]
            stacked[rows + at : rows + at + 1, 0:atoms] += mom[b, c : c + 1, :]
    shares = jnp.dot(
        maps[lax.axis_index("bead")],
        stacked[...],
        precision=lax.Precision.HIGHEST,
        preferred_element_type=f32,
    )
    for at, out in enumerate(outs):
        out[...] = shares[at * 2 * rows : (at + 1) * 2 * rows, 0:atoms]


def on_device(
    positions, momenta, neighbours, nbr_count, send_rows, embed_first, embed_weight,
    embed_bias, fit_weight, fit_bias, fit_weight2, fit_bias2, fit_out,
):
    bead_dev, comps, atoms = positions.shape
    listed = neighbours.shape[1]
    wide, fit = fit_weight.shape
    emb = embed_weight.shape[0]
    fit_pad = -(-fit // LANES) * LANES
    rows = bead_dev * comps
    blocks = atoms // GROUP
    width = GROUP * listed
    many = bead_dev * atoms
    shape = jax.ShapeDtypeStruct
    big = pltpu.CompilerParams(vmem_limit_bytes=50 * 1024 * 1024)

    domains = lax.axis_size("space")
    pairs = [(d, d + 1) for d in range(0, domains - 1, 2)]
    links = [(d, d + 1) for d in range(1, domains - 1, 2)]

    def swapped(value, which):
        return lax.ppermute(value, "space", which + [(b, a) for a, b in which])

    own = jnp.concatenate(
        [positions.transpose(1, 0, 2).reshape(rows, atoms), send_rows[0].astype(f32)], axis=0
    )
    core = swapped(own, pairs)
    link = swapped(jnp.concatenate([own, core], axis=0), links)
    far = swapped(link, pairs)

    w_embed_t, fit_rows, fit_cols, fit_w2, fit_w2t, columns, fit_columns = pl.pallas_call(
        prepare_kernel,
        out_shape=[
            shape((emb, emb), bf16),
            shape((wide, fit_pad), bf16),
            shape((fit_pad, wide), bf16),
            shape((fit_pad, fit_pad), bf16),
            shape((fit_pad, fit_pad), bf16),
            shape((3, emb, LANES), f32),
            shape((3, fit_pad, LANES), f32),
        ],
        compiler_params=big,
        cost_estimate=pl.CostEstimate(
            flops=2 * wide * fit_pad * (LANES + fit_pad), bytes_accessed=8 * wide * fit_pad, transcendentals=0
        ),
        name="weights",
    )(
        embed_first, embed_weight, embed_bias.reshape(1, emb), fit_weight,
        fit_bias.reshape(1, fit), fit_weight2, fit_bias2.reshape(1, fit), fit_out.reshape(1, fit),
    )
    vmem = pl.BlockSpec(memory_space=pltpu.VMEM)
    anywhere = pl.BlockSpec(memory_space=pl.ANY)
    own_f, near_f, link_f = pl.pallas_call(
        force_kernel,
        out_shape=[shape((rows, atoms), f32), shape((2 * rows, atoms), f32), shape((2 * rows, atoms), f32)],
        in_specs=[vmem] * 7 + [anywhere] * 2 + [vmem] * 4,
        scratch_shapes=[
            pltpu.VMEM((5, comps, 8, LANES), f32),
            pltpu.VMEM((8, LANES), jnp.int32),
            pltpu.VMEM((4, 8, LANES), jnp.int32),
            pltpu.VMEM((4, blocks, 8, width), f32),
            pltpu.VMEM((blocks, 8, width), f32),
            pltpu.VMEM((comps, blocks, 8, width), f32),
            pltpu.VMEM((bead_dev * blocks, emb, width), bf16),
            pltpu.VMEM((bead_dev * blocks, emb, width), bf16),
            pltpu.VMEM((4, many, emb), f32),
            pltpu.VMEM((4, emb, many), f32),
            pltpu.VMEM((wide, many), bf16),
            pltpu.VMEM((wide, many), f32),
            pltpu.VMEM((4, emb, many), f32),
            pltpu.VMEM((4, many, emb), f32),
            pltpu.VMEM((5, 8, width), f32),
            pltpu.VMEM((5 * LANES, LANES), f32),
            pltpu.VMEM((blocks, 8, width), jnp.int32),
            pltpu.VMEM((wide, fit_pad), bf16),
            pltpu.VMEM((fit_pad, wide), bf16),
            pltpu.SemaphoreType.DMA((2,)),
        ],
        compiler_params=big,
        name="forces",
    )(
        own, core, link, far, neighbours.reshape(blocks, width), nbr_count.reshape(1, atoms),
        w_embed_t, fit_rows, fit_cols, columns, fit_columns, fit_w2, fit_w2t,
    )
    near = swapped(near_f, pairs)
    link = swapped(
        jnp.concatenate([link_f[:rows] + near[rows:], link_f[rows:]], axis=0), links
    )
    far = swapped(link, pairs)

    groups = lax.axis_size("bead")
    maps = jnp.asarray(propagation_table(groups, bead_dev))
    shares = pl.pallas_call(
        finish_kernel,
        out_shape=[shape((2 * rows, atoms), f32)] * groups,
        scratch_shapes=[pltpu.VMEM((LANES, LANES), f32)],
        name="propagate",
    )(positions, momenta, own_f, near, link, far, maps)
    if groups == 2:
        result = shares[0] + lax.ppermute(shares[1], "bead", [(0, 1), (1, 0)])
    else:
        parts = lax.all_to_all(jnp.stack(shares), "bead", split_axis=0, concat_axis=0, tiled=True)
        result = parts.sum(axis=0)
    return (result[:rows].reshape(positions.shape), result[rows:].reshape(positions.shape))


def solution(mesh):
    in_specs = (
        P("bead", None, "space"),
        P("bead", None, "space"),
        P("space", None),
        P("space"),
        P("space", None, None),
    ) + (P(),) * 8
    out_specs = (P("bead", None, "space"), P("bead", None, "space"))
    return jax.shard_map(
        on_device, mesh=mesh, in_specs=in_specs, out_specs=out_specs, check_vma=False
    )
```

```python
import functools

import jax
import jax.numpy as jnp
import numpy as np
from jax import lax
from jax.experimental import pallas as pl
from jax.experimental.pallas import tpu as pltpu
from jax.sharding import PartitionSpec as P

AXIS = 16
LANES = 128
GROUP = 8

cycle_freq = 0.5
time_step = 1.0
soften = 0.25
force_gain = 64.0

f32 = jnp.float32
bf16 = jnp.bfloat16


def passed_along(value, axis, steps):
    count = lax.axis_size(axis)
    first, last = (max(0, -steps), min(count, count - steps))
    return lax.ppermute(value, axis, [(source, source + steps) for source in range(first, last)])


def mode_maps(beads):
    column = np.arange(beads)[None, :]
    bead_row = np.arange(beads)[:, None]
    phases = 2.0 * np.pi * bead_row * column / beads
    mode_basis = np.where(
        column == 0,
        1.0 / np.sqrt(beads),
        np.where(
            2 * column < beads,
            np.sqrt(2.0 / beads) * np.cos(phases),
            np.where(
                2 * column == beads,
                np.cos(phases) / np.sqrt(beads),
                np.sqrt(2.0 / beads) * np.sin(phases),
            ),
        ),
    )
    frequency = 2.0 * cycle_freq * np.sin(np.pi * np.arange(beads) / beads)
    angles = frequency * time_step
    safe_freq = np.where(frequency > 0, frequency, 1.0)
    cosine = np.cos(angles)
    drift = np.where(frequency > 0, np.sin(angles) / safe_freq, time_step)
    pull = -frequency * np.sin(angles)
    keep_map = mode_basis * cosine[None, :] @ mode_basis.T
    drift_map = mode_basis * drift[None, :] @ mode_basis.T
    pull_map = mode_basis * pull[None, :] @ mode_basis.T
    return keep_map, drift_map, pull_map


def propagation_table(groups, bead_dev):
    keep, drift, pull = mode_maps(groups * bead_dev)
    table = np.zeros((groups, groups, 2, 3, bead_dev, 2, 3, bead_dev))
    for source in range(groups):
        cols = slice(source * bead_dev, (source + 1) * bead_dev)
        for target in range(groups):
            rows = slice(target * bead_dev, (target + 1) * bead_dev)
            for c in range(3):
                table[source, target, 0, c, :, 0, c, :] = keep[rows, cols]
                table[source, target, 0, c, :, 1, c, :] = drift[rows, cols]
                table[source, target, 1, c, :, 0, c, :] = pull[rows, cols]
                table[source, target, 1, c, :, 1, c, :] = keep[rows, cols]
    if groups == 2:
        table[1] = table[1, ::-1].copy()
    table = table.reshape(groups, groups * 6 * bead_dev, 6 * bead_dev)
    return np.pad(table, ((0, 0), (0, 0), (0, LANES - table.shape[2]))).astype(np.float32)


def lane_take(values, picked):
    numbers = lax.GatherDimensionNumbers(
        offset_dims=(),
        collapsed_slice_dims=(1,),
        start_index_map=(1,),
        operand_batching_dims=(0,),
        start_indices_batching_dims=(0,),
    )
    return lax.gather(
        values,
        picked[..., None],
        numbers,
        (1, 1),
        mode=lax.GatherScatterMode.PROMISE_IN_BOUNDS,
    )


def dot(a, b):
    return jnp.dot(a, b, preferred_element_type=f32)


def dot_nt(a, b):
    return lax.dot_general(a, b, (((1,), (1,)), ((), ())), preferred_element_type=f32)


def column_of(row, rows):
    wide = jnp.broadcast_to(row, (LANES, rows))
    return jnp.transpose(wide)


def wide_columns(column, width):
    return jnp.concatenate([column] * (width // LANES), axis=1)


def split_dot(a, b):
    high = b.astype(bf16)
    return dot(a, high) + dot(a, (b - high.astype(f32)).astype(bf16))


def pack_kernel(pos, mom, send, out, mom_out):
    comps, beads, _ = pos.shape
    for c in range(comps):
        out[c * beads : (c + 1) * beads, :] = pos[c]
        mom_out[c * beads : (c + 1) * beads, :] = mom[c]
    out[comps * beads : comps * beads + send.shape[1], :] = send[0].astype(f32)


def unit(n):
    same = lax.broadcasted_iota(jnp.int32, (n, n), 0) == lax.broadcasted_iota(jnp.int32, (n, n), 1)
    return jnp.where(same, 1.0, 0.0).astype(bf16)


def force_kernel(
    own, mom, core, link, far, idx, cnt, first, w_embed, e_bias, fit_t, f_bias, fit_w2, f_bias2, f_out,
    own_f, near_f, link_f,
    table, counts, sent, radial, inverse, offset, second, slope,
    moment, moment_t, desc, d_desc, d_moment_t, d_moment, pair_grad, totals, index,
    fit_here, rows_here, cols_here, w_embed_t, w2_here, w2_t, columns, fit_columns, loaded,
):
    beads = 4
    comps = 3
    atoms = own.shape[1]
    blocks, width = idx.shape
    listed = width // GROUP
    emb = w_embed.shape[0]
    fit, wide = fit_t.shape
    fit_pad = rows_here.shape[1]
    rows = beads * comps
    load = pltpu.make_async_copy(fit_t, fit_here, loaded)
    load.start()

    odd = lax.rem(lax.axis_index("space"), 2) == 1
    block_of = ((2, 1), (1, 2), (0, 3), (3, 0))
    table[...] = jnp.zeros_like(table)
    sent[...] = jnp.zeros_like(sent)
    sources = ((own, 0), (core, 0), (link, 0), (link, link.shape[0] // 2), (far, 0))
    for role, (source, at) in enumerate(sources):
        for c in range(comps):
            table[role, c, 0:beads, 0:atoms] = source[at + c * beads : at + (c + 1) * beads, :]
        if role > 0:
            if_odd, if_even = (
                source[at + rows + j : at + rows + j + 1, :] for j in block_of[role - 1]
            )
            row = jnp.maximum(jnp.where(odd, if_odd, if_even), 0.0).astype(jnp.int32)
            sent[role - 1, :, 0:atoms] = jnp.broadcast_to(row, (8, atoms))
    role_of = [
        jnp.where(odd, 1 + [pair[0] for pair in block_of].index(j), 1 + [pair[1] for pair in block_of].index(j))
        for j in range(4)
    ]
    counts[...] = jnp.zeros_like(counts)
    counts[:, 0:atoms] = jnp.broadcast_to(cnt[...], (8, atoms))
    pair_grad[...] = jnp.zeros_like(pair_grad)
    totals[...] = jnp.zeros_like(totals)
    for i in range(blocks):
        index[i] = jnp.broadcast_to(idx[i : i + 1, :], (8, width))

    columns[0] = column_of(first[0:1, :], emb)
    columns[1] = column_of(first[1:2, :], emb)
    columns[2] = column_of(e_bias[...], emb)
    for at, vector in enumerate((f_bias, f_bias2, f_out)):
        pad = jnp.zeros((1, fit_pad - fit), f32)
        fit_columns[at] = column_of(jnp.concatenate([vector[...], pad], axis=1), fit_pad)
    w_embed_t[...] = dot_nt(unit(emb), w_embed[...]).astype(bf16)
    w2_here[...] = jnp.zeros_like(w2_here)
    w2_here[0:fit, 0:fit] = fit_w2[...]
    w2_t[...] = dot_nt(unit(fit_pad), w2_here[...]).astype(bf16)
    cols_here[fit:fit_pad, :] = jnp.zeros((fit_pad - fit, wide), bf16)
    row = lax.broadcasted_iota(jnp.int32, (LANES, LANES), 0)
    source = AXIS * (row % 8) + row // 8
    order = jnp.where(lax.broadcasted_iota(jnp.int32, (LANES, LANES), 1) == source, 1.0, 0.0).astype(bf16)
    blank = jnp.zeros((LANES, fit_pad - fit), f32)
    chunks = wide // LANES
    each = -(-chunks // blocks)
    load.wait()

    lane = lax.broadcasted_iota(jnp.int32, (8, LANES), 1)

    def pairs(i, carry):
        for turn in range(each):
            chunk = jnp.minimum(each * i + turn, chunks - 1)
            part = pl.ds(pl.multiple_of(chunk * LANES, LANES), LANES)
            chunk_t = fit_here[:, part]
            rows_here[part, :] = jnp.concatenate([dot_nt(order, chunk_t), blank], axis=1).astype(bf16)
            cols_here[0:fit, part] = dot_nt(chunk_t, order).astype(bf16)
        for part in range(width // LANES):
            cols = slice(part * LANES, (part + 1) * LANES)
            ix = index[i, :, cols]
            atom = GROUP * i + part * (LANES // listed) + lane // listed
            entry = lane % listed
            role = jnp.where(ix >= atoms, role_of[0], 0)
            block = jnp.where(ix >= atoms, 1, 0)
            for j in range(1, 4):
                role = jnp.where(ix >= (j + 1) * atoms, role_of[j], role)
                block = jnp.where(ix >= (j + 1) * atoms, j + 1, block)
            slot = ix - atoms * block
            local = slot
            for r in range(1, 5):
                local = jnp.where(role == r, lane_take(sent[r - 1], slot), local)
            index[i, :, cols] = local + role * LANES
            active = entry < lane_take(counts[...], atom)
            offs = []
            for c in range(comps):
                near = lane_take(table[0, c], local)
                for j in range(1, len(sources)):
                    near = jnp.where(role == j, lane_take(table[j, c], local), near)
                offs.append(near - lane_take(table[0, c], atom))
            square = offs[0] * offs[0] + offs[1] * offs[1] + offs[2] * offs[2]
            inv = lax.rsqrt(square + soften)
            smooth = jnp.where(active, inv, 0.0)
            scaled = smooth * inv
            inverse[i, :, cols] = inv
            radial[0, i, :, cols] = smooth
            for c in range(comps):
                offset[c, i, :, cols] = offs[c]
                radial[c + 1, i, :, cols] = scaled * offs[c]
        return carry

    lax.fori_loop(0, blocks, pairs, 0)

    segment = (
        lax.broadcasted_iota(jnp.int32, (GROUP, width), 1) // listed
        == lax.broadcasted_iota(jnp.int32, (GROUP, width), 0)
    )

    def embed(i, carry):
        for b in range(beads):
            w_first = wide_columns(columns[0], width)
            smooth = radial[0, i, b : b + 1, :]
            one = jnp.tanh(smooth * w_first + wide_columns(columns[1], width))
            one_slope = (1.0 - one * one) * w_first
            low = jnp.concatenate([one.astype(bf16), one_slope.astype(bf16)], axis=1)
            product = dot(w_embed_t[...], low)
            two = jnp.tanh(product[:, 0:width] + wide_columns(columns[2], width))
            both = one + two
            total = both.astype(bf16)
            second[b * blocks + i] = total
            slope[b * blocks + i] = (one_slope + (1.0 - two * two) * product[:, width:]).astype(bf16)
            spread = jnp.concatenate(
                [jnp.where(segment, radial[x, i, b : b + 1, :], 0.0) for x in range(4)], axis=0
            )
            high = spread.astype(bf16)
            halves = jnp.concatenate([high, (spread - high.astype(f32)).astype(bf16)], axis=0)
            part = dot_nt(halves, total)
            rest = dot_nt(high, (both - total.astype(f32)).astype(bf16))
            part = (part[0 : 4 * GROUP, :] + part[4 * GROUP :, :] + rest) * (1.0 / listed)
            start = pl.multiple_of(b * atoms + GROUP * i, GROUP)
            for x in range(4):
                moment[x, pl.ds(start, GROUP), :] = part[x * GROUP : (x + 1) * GROUP, :]
        return carry

    lax.fori_loop(0, blocks, embed, 0)

    for x in range(4):
        moment_t[x] = jnp.transpose(moment[x])
    def describe(e, carry):
        mine = [moment_t[x, pl.ds(pl.multiple_of(e * 8, 8), 8), :] for x in range(4)]
        for f in range(0, AXIS, 2):
            values = []
            for g in (f, f + 1):
                value = mine[0] * moment_t[0, g : g + 1, :]
                for x in range(1, 4):
                    value += mine[x] * moment_t[x, g : g + 1, :]
                values.append(value)
            at = pl.ds(pl.multiple_of(e * 8 * AXIS + f * 8, 16), 16)
            desc[at, :] = jnp.concatenate(values, axis=0).astype(bf16)
        return carry

    lax.fori_loop(0, emb // 8, describe, 0)
    many = beads * atoms
    bias, bias2, out_col = (wide_columns(fit_columns[at], many) for at in range(3))
    hidden = jnp.tanh(dot(cols_here[...], desc[...]) + bias)
    more = jnp.tanh(dot(w2_t[...], hidden.astype(bf16)) + bias2)
    d_more = out_col * (1.0 - more * more)
    d_hidden = out_col + split_dot(w2_here[...], d_more).astype(bf16).astype(f32)
    d_pre = d_hidden * (1.0 - hidden * hidden)
    d_desc[...] = split_dot(rows_here[...], d_pre).astype(bf16).astype(f32)

    def left(e, carry):
        rows = pl.ds(pl.multiple_of(e * 8, 8), 8)
        sums = [None] * 4
        for f in range(AXIS):
            grad = d_desc[pl.ds(pl.multiple_of((e * AXIS + f) * 8, 8), 8), :]
            for x in range(4):
                term = grad * moment_t[x, f : f + 1, :]
                sums[x] = term if f == 0 else sums[x] + term
        for x in range(4):
            d_moment_t[x, rows, :] = sums[x]
        return carry

    lax.fori_loop(0, emb // 8, left, 0)
    for f in range(AXIS):
        terms = [None] * 4
        for e in range(emb // 8):
            grad = d_desc[(e * AXIS + f) * 8 : (e * AXIS + f + 1) * 8, :]
            for x in range(4):
                term = grad * moment_t[x, e * 8 : (e + 1) * 8, :]
                terms[x] = term if e == 0 else terms[x] + term
        for x in range(4):
            d_moment_t[x, f : f + 1, :] += jnp.sum(terms[x], axis=0, keepdims=True)
    for x in range(4):
        d_moment[x] = jnp.transpose(d_moment_t[x]) * (1.0 / listed)

    row_of = lax.broadcasted_iota(jnp.int32, (atoms, width), 0)
    lane_of = lax.broadcasted_iota(jnp.int32, (atoms, width), 1)

    def backward(i, carry):
        for b in range(beads):
            start = pl.multiple_of(b * atoms + GROUP * i, GROUP)
            left_side = jnp.concatenate(
                [d_moment[x, pl.ds(start, GROUP), :] for x in range(4)], axis=0
            )
            high = left_side.astype(bf16)
            halves = jnp.concatenate([high, (left_side - high.astype(f32)).astype(bf16)], axis=0)
            by_second = dot(halves, second[b * blocks + i])
            by_second = by_second[0 : 4 * GROUP, :] + by_second[4 * GROUP :, :]
            by_slope = dot(halves, slope[b * blocks + i])
            by_slope = by_slope[0 : 4 * GROUP, :] + by_slope[4 * GROUP :, :]
            along = None
            for x in range(4):
                rows = slice(x * GROUP, (x + 1) * GROUP)
                pair_grad[x, b : b + 1, :] = jnp.sum(
                    jnp.where(segment, by_second[rows, :], 0.0), axis=0, keepdims=True
                )
                term = by_slope[rows, :] * radial[x, i, b : b + 1, :]
                along = term if along is None else along + term
            pair_grad[4, b : b + 1, :] = jnp.sum(
                jnp.where(segment, along, 0.0), axis=0, keepdims=True
            )
        inv = inverse[i]
        smooth = radial[0, i]
        offs = [offset[c, i] for c in range(comps)]
        along = pair_grad[1] * offs[0] + pair_grad[2] * offs[1] + pair_grad[3] * offs[2]
        live = jnp.where(smooth > 0.0, 1.0, 0.0)
        d_inv = live * (pair_grad[0] + pair_grad[4]) + 2.0 * smooth * along
        pull = d_inv * inv * inv * inv
        scaled = smooth * inv
        grads = [pair_grad[c + 1] * scaled - pull * offs[c] for c in range(comps)]
        high = [g.astype(bf16) for g in grads]
        low = [(g - h.astype(f32)) for g, h in zip(grads, high)]
        sides = jnp.concatenate(
            [h.astype(f32) for h in high] + low, axis=0
        ).astype(bf16)
        ix = index[i, 0:1, :]
        for j in range(len(sources)):
            hot = jnp.where(row_of == ix - j * LANES, 1.0, 0.0)
            if j == 0:
                hot = hot - jnp.where(row_of == GROUP * i + lane_of // listed, 1.0, 0.0)
            totals[j * LANES : j * LANES + atoms, 0 : 6 * 8] += dot_nt(hot.astype(bf16), sides)
        return carry

    lax.fori_loop(0, blocks, backward, 0)

    targets = ((own_f, 0), (near_f, 0), (link_f, 0), (link_f, rows), (near_f, rows))
    for j, (out, at) in enumerate(targets):
        turned = jnp.transpose(totals[j * LANES : (j + 1) * LANES, :])
        whole = turned[0:24, :] + turned[24:48, :]
        for c in range(comps):
            value = -whole[c * 8 : c * 8 + beads, 0:atoms]
            if j == 0:
                value = mom[c * beads : (c + 1) * beads, :] + (time_step * force_gain) * value
            out[at + c * beads : at + (c + 1) * beads, :] = value


def finish_kernel(own, kicked, near, link, far, maps, *outs_and_scratch):
    outs, stacked = outs_and_scratch[:-1], outs_and_scratch[-1]
    rows, atoms = kicked.shape
    force = near[0:rows, :] + (link[0:rows, :] + far[rows : 2 * rows, :])
    stacked[...] = jnp.zeros_like(stacked)
    stacked[0:rows, 0:atoms] = own[0:rows, :]
    stacked[rows : 2 * rows, 0:atoms] = kicked[...] + force * (time_step * force_gain)
    shares = jnp.dot(
        maps[lax.axis_index("bead")],
        stacked[...],
        precision=lax.Precision.HIGHEST,
        preferred_element_type=f32,
    )
    for at, out in enumerate(outs):
        for k in range(out.shape[0]):
            start = at * 2 * rows + k * out.shape[1]
            out[k] = shares[start : start + out.shape[1], 0:atoms]


def on_device(
    positions, momenta, neighbours, nbr_count, send_rows, embed_first, embed_weight,
    embed_bias, fit_weight, fit_bias, fit_weight2, fit_bias2, fit_out,
):
    bead_dev, comps, atoms = positions.shape
    listed = neighbours.shape[1]
    wide, fit = fit_weight.shape
    emb = embed_weight.shape[0]
    fit_pad = -(-fit // LANES) * LANES
    rows = bead_dev * comps
    blocks = atoms // GROUP
    width = GROUP * listed
    many = bead_dev * atoms
    shape = jax.ShapeDtypeStruct
    big = pltpu.CompilerParams(vmem_limit_bytes=50 * 1024 * 1024)

    vmem = pl.BlockSpec(memory_space=pltpu.VMEM)
    anywhere = pl.BlockSpec(memory_space=pl.ANY)

    domains = lax.axis_size("space")
    pairs = [(d, d + 1) for d in range(0, domains - 1, 2)]
    links = [(d, d + 1) for d in range(1, domains - 1, 2)]

    def swapped(value, which):
        return lax.ppermute(value, "space", which + [(b, a) for a, b in which])

    send_blocks = send_rows.shape[1]
    own, momenta_rows = pl.pallas_call(
        pack_kernel,
        out_shape=[shape((rows + send_blocks, atoms), f32), shape((rows, atoms), f32)],
        in_specs=[vmem] * 3,
        out_specs=[vmem] * 2,
        name="pack",
    )(positions.transpose(1, 0, 2), momenta.transpose(1, 0, 2), send_rows)
    core = swapped(own, pairs)
    link = swapped(jnp.concatenate([own, core], axis=0), links)
    far = swapped(link, pairs)

    own_f, near_f, link_f = pl.pallas_call(
        force_kernel,
        out_shape=[shape((rows, atoms), f32), shape((2 * rows, atoms), f32), shape((2 * rows, atoms), f32)],
        in_specs=[vmem] * 10 + [anywhere] + [vmem] * 4,
        out_specs=[vmem] * 3,
        scratch_shapes=[
            pltpu.VMEM((5, comps, 8, LANES), f32),
            pltpu.VMEM((8, LANES), jnp.int32),
            pltpu.VMEM((4, 8, LANES), jnp.int32),
            pltpu.VMEM((4, blocks, 8, width), f32),
            pltpu.VMEM((blocks, 8, width), f32),
            pltpu.VMEM((comps, blocks, 8, width), f32),
            pltpu.VMEM((bead_dev * blocks, emb, width), bf16),
            pltpu.VMEM((bead_dev * blocks, emb, width), bf16),
            pltpu.VMEM((4, many, emb), f32),
            pltpu.VMEM((4, emb, many), f32),
            pltpu.VMEM((wide, many), bf16),
            pltpu.VMEM((wide, many), f32),
            pltpu.VMEM((4, emb, many), f32),
            pltpu.VMEM((4, many, emb), f32),
            pltpu.VMEM((5, 8, width), f32),
            pltpu.VMEM((5 * LANES, LANES), f32),
            pltpu.VMEM((blocks, 8, width), jnp.int32),
            pltpu.VMEM((fit, wide), bf16),
            pltpu.VMEM((wide, fit_pad), bf16),
            pltpu.VMEM((fit_pad, wide), bf16),
            pltpu.VMEM((emb, emb), bf16),
            pltpu.VMEM((fit_pad, fit_pad), bf16),
            pltpu.VMEM((fit_pad, fit_pad), bf16),
            pltpu.VMEM((3, emb, LANES), f32),
            pltpu.VMEM((3, fit_pad, LANES), f32),
            pltpu.SemaphoreType.DMA(()),
        ],
        compiler_params=big,
        name="forces",
    )(
        own, momenta_rows, core, link, far, neighbours.reshape(blocks, width), nbr_count.reshape(1, atoms),
        embed_first, embed_weight, embed_bias.reshape(1, emb), fit_weight.T,
        fit_bias.reshape(1, fit), fit_weight2, fit_bias2.reshape(1, fit), fit_out.reshape(1, fit),
    )
    near = swapped(near_f, pairs)
    link = swapped(
        jnp.concatenate([link_f[:rows] + near[rows:], link_f[rows:]], axis=0), links
    )
    far = swapped(link, pairs)

    groups = lax.axis_size("bead")
    maps = jnp.asarray(propagation_table(groups, bead_dev))
    shares = pl.pallas_call(
        finish_kernel,
        out_shape=[shape((2 * comps, bead_dev, atoms), f32)] * groups,
        in_specs=[vmem] * 6,
        out_specs=[vmem] * groups,
        scratch_shapes=[pltpu.VMEM((LANES, LANES), f32)],
        name="propagate",
    )(own, own_f, near, link, far, maps)
    if groups == 2:
        result = shares[0] + lax.ppermute(shares[1], "bead", [(0, 1), (1, 0)])
    else:
        parts = lax.all_to_all(jnp.stack(shares), "bead", split_axis=0, concat_axis=0, tiled=True)
        result = parts.sum(axis=0)
    return (result[:comps].transpose(1, 0, 2), result[comps:].transpose(1, 0, 2))


def solution(mesh):
    in_specs = (
        P("bead", None, "space"),
        P("bead", None, "space"),
        P("space", None),
        P("space"),
        P("space", None, None),
    ) + (P(),) * 8
    out_specs = (P("bead", None, "space"), P("bead", None, "space"))
    return jax.shard_map(
        on_device, mesh=mesh, in_specs=in_specs, out_specs=out_specs, check_vma=False
    )
```

```python
import functools

import jax
import jax.numpy as jnp
import numpy as np
from jax import lax
from jax.experimental import pallas as pl
from jax.experimental.pallas import tpu as pltpu
from jax.sharding import PartitionSpec as P

AXIS = 16
LANES = 128
GROUP = 8

cycle_freq = 0.5
time_step = 1.0
soften = 0.25
force_gain = 64.0

f32 = jnp.float32
bf16 = jnp.bfloat16


def passed_along(value, axis, steps):
    count = lax.axis_size(axis)
    first, last = (max(0, -steps), min(count, count - steps))
    return lax.ppermute(value, axis, [(source, source + steps) for source in range(first, last)])


def mode_maps(beads):
    column = np.arange(beads)[None, :]
    bead_row = np.arange(beads)[:, None]
    phases = 2.0 * np.pi * bead_row * column / beads
    mode_basis = np.where(
        column == 0,
        1.0 / np.sqrt(beads),
        np.where(
            2 * column < beads,
            np.sqrt(2.0 / beads) * np.cos(phases),
            np.where(
                2 * column == beads,
                np.cos(phases) / np.sqrt(beads),
                np.sqrt(2.0 / beads) * np.sin(phases),
            ),
        ),
    )
    frequency = 2.0 * cycle_freq * np.sin(np.pi * np.arange(beads) / beads)
    angles = frequency * time_step
    safe_freq = np.where(frequency > 0, frequency, 1.0)
    cosine = np.cos(angles)
    drift = np.where(frequency > 0, np.sin(angles) / safe_freq, time_step)
    pull = -frequency * np.sin(angles)
    keep_map = mode_basis * cosine[None, :] @ mode_basis.T
    drift_map = mode_basis * drift[None, :] @ mode_basis.T
    pull_map = mode_basis * pull[None, :] @ mode_basis.T
    return keep_map, drift_map, pull_map


def propagation_table(groups, bead_dev):
    keep, drift, pull = mode_maps(groups * bead_dev)
    table = np.zeros((groups, groups, 2, 3, bead_dev, 2, 3, bead_dev))
    for source in range(groups):
        cols = slice(source * bead_dev, (source + 1) * bead_dev)
        for target in range(groups):
            rows = slice(target * bead_dev, (target + 1) * bead_dev)
            for c in range(3):
                table[source, target, 0, c, :, 0, c, :] = keep[rows, cols]
                table[source, target, 0, c, :, 1, c, :] = drift[rows, cols]
                table[source, target, 1, c, :, 0, c, :] = pull[rows, cols]
                table[source, target, 1, c, :, 1, c, :] = keep[rows, cols]
    if groups == 2:
        table[1] = table[1, ::-1].copy()
    table = table.reshape(groups, groups * 6 * bead_dev, 6 * bead_dev)
    return np.pad(table, ((0, 0), (0, 0), (0, LANES - table.shape[2]))).astype(np.float32)


def lane_take(values, picked):
    numbers = lax.GatherDimensionNumbers(
        offset_dims=(),
        collapsed_slice_dims=(1,),
        start_index_map=(1,),
        operand_batching_dims=(0,),
        start_indices_batching_dims=(0,),
    )
    return lax.gather(
        values,
        picked[..., None],
        numbers,
        (1, 1),
        mode=lax.GatherScatterMode.PROMISE_IN_BOUNDS,
    )


def dot(a, b):
    return jnp.dot(a, b, preferred_element_type=f32)


def dot_nt(a, b):
    return lax.dot_general(a, b, (((1,), (1,)), ((), ())), preferred_element_type=f32)


def column_of(row, rows):
    wide = jnp.broadcast_to(row, (LANES, rows))
    return jnp.transpose(wide)


def wide_columns(column, width):
    return jnp.concatenate([column] * (width // LANES), axis=1)


def split_dot(a, b):
    high = b.astype(bf16)
    return dot(a, high) + dot(a, (b - high.astype(f32)).astype(bf16))


def pack_kernel(pos, send, out):
    comps, beads, _ = pos.shape
    for c in range(comps):
        out[c * beads : (c + 1) * beads, :] = pos[c]
    out[comps * beads : comps * beads + send.shape[1], :] = send[0].astype(f32)


def unit(n):
    same = lax.broadcasted_iota(jnp.int32, (n, n), 0) == lax.broadcasted_iota(jnp.int32, (n, n), 1)
    return jnp.where(same, 1.0, 0.0).astype(bf16)


def force_kernel(
    own, mom, core, link, far, idx, cnt, first, w_embed, e_bias, fit_t, f_bias, fit_w2, f_bias2, f_out,
    own_f, near_f, link_f,
    table, counts, sent, radial, inverse, offset, second, slope,
    moment, moment_t, desc, d_desc, d_moment_t, d_moment, pair_grad, totals, index,
    rows_here, cols_here, w_embed_t, w2_here, w2_t, columns, fit_columns,
):
    beads = 4
    comps = 3
    atoms = own.shape[1]
    blocks, width = idx.shape
    listed = width // GROUP
    emb = w_embed.shape[0]
    fit, wide = fit_t.shape
    fit_pad = rows_here.shape[1]
    rows = beads * comps
    odd = lax.rem(lax.axis_index("space"), 2) == 1
    block_of = ((2, 1), (1, 2), (0, 3), (3, 0))
    table[...] = jnp.zeros_like(table)
    sent[...] = jnp.zeros_like(sent)
    sources = ((own, 0), (core, 0), (link, 0), (link, link.shape[0] // 2), (far, 0))
    for role, (source, at) in enumerate(sources):
        for c in range(comps):
            table[role, c, 0:beads, 0:atoms] = source[at + c * beads : at + (c + 1) * beads, :]
        if role > 0:
            if_odd, if_even = (
                source[at + rows + j : at + rows + j + 1, :] for j in block_of[role - 1]
            )
            row = jnp.maximum(jnp.where(odd, if_odd, if_even), 0.0).astype(jnp.int32)
            sent[role - 1, :, 0:atoms] = jnp.broadcast_to(row, (8, atoms))
    role_of = [
        jnp.where(odd, 1 + [pair[0] for pair in block_of].index(j), 1 + [pair[1] for pair in block_of].index(j))
        for j in range(4)
    ]
    counts[...] = jnp.zeros_like(counts)
    counts[:, 0:atoms] = jnp.broadcast_to(cnt[...], (8, atoms))
    pair_grad[...] = jnp.zeros_like(pair_grad)
    totals[...] = jnp.zeros_like(totals)
    for i in range(blocks):
        index[i] = jnp.broadcast_to(idx[i : i + 1, :], (8, width))

    columns[0] = column_of(first[0:1, :], emb)
    columns[1] = column_of(first[1:2, :], emb)
    columns[2] = column_of(e_bias[...], emb)
    for at, vector in enumerate((f_bias, f_bias2, f_out)):
        pad = jnp.zeros((1, fit_pad - fit), f32)
        fit_columns[at] = column_of(jnp.concatenate([vector[...], pad], axis=1), fit_pad)
    w_embed_t[...] = dot_nt(unit(emb), w_embed[...]).astype(bf16)
    w2_here[...] = jnp.zeros_like(w2_here)
    w2_here[0:fit, 0:fit] = fit_w2[...]
    w2_t[...] = dot_nt(unit(fit_pad), w2_here[...]).astype(bf16)
    cols_here[fit:fit_pad, :] = jnp.zeros((fit_pad - fit, wide), bf16)
    row = lax.broadcasted_iota(jnp.int32, (LANES, LANES), 0)
    source = AXIS * (row % 8) + row // 8
    order = jnp.where(lax.broadcasted_iota(jnp.int32, (LANES, LANES), 1) == source, 1.0, 0.0).astype(bf16)
    blank = jnp.zeros((LANES, fit_pad - fit), f32)
    chunks = wide // LANES
    each = -(-chunks // blocks)

    lane = lax.broadcasted_iota(jnp.int32, (8, LANES), 1)

    def pairs(i, carry):
        for turn in range(each):
            chunk = jnp.minimum(each * i + turn, chunks - 1)
            part = pl.ds(pl.multiple_of(chunk * LANES, LANES), LANES)
            chunk_t = fit_t[:, part]
            rows_here[part, :] = jnp.concatenate([dot_nt(order, chunk_t), blank], axis=1).astype(bf16)
            cols_here[0:fit, part] = dot_nt(chunk_t, order).astype(bf16)
        for part in range(width // LANES):
            cols = slice(part * LANES, (part + 1) * LANES)
            ix = index[i, :, cols]
            atom = GROUP * i + part * (LANES // listed) + lane // listed
            entry = lane % listed
            role = jnp.where(ix >= atoms, role_of[0], 0)
            block = jnp.where(ix >= atoms, 1, 0)
            for j in range(1, 4):
                role = jnp.where(ix >= (j + 1) * atoms, role_of[j], role)
                block = jnp.where(ix >= (j + 1) * atoms, j + 1, block)
            slot = ix - atoms * block
            local = slot
            for r in range(1, 5):
                local = jnp.where(role == r, lane_take(sent[r - 1], slot), local)
            index[i, :, cols] = local + role * LANES
            active = entry < lane_take(counts[...], atom)
            offs = []
            for c in range(comps):
                near = lane_take(table[0, c], local)
                for j in range(1, len(sources)):
                    near = jnp.where(role == j, lane_take(table[j, c], local), near)
                offs.append(near - lane_take(table[0, c], atom))
            square = offs[0] * offs[0] + offs[1] * offs[1] + offs[2] * offs[2]
            inv = lax.rsqrt(square + soften)
            smooth = jnp.where(active, inv, 0.0)
            scaled = smooth * inv
            inverse[i, :, cols] = inv
            radial[0, i, :, cols] = smooth
            for c in range(comps):
                offset[c, i, :, cols] = offs[c]
                radial[c + 1, i, :, cols] = scaled * offs[c]
        return carry

    lax.fori_loop(0, blocks, pairs, 0)

    segment = (
        lax.broadcasted_iota(jnp.int32, (GROUP, width), 1) // listed
        == lax.broadcasted_iota(jnp.int32, (GROUP, width), 0)
    )

    def embed(i, carry):
        for b in range(beads):
            w_first = wide_columns(columns[0], width)
            smooth = radial[0, i, b : b + 1, :]
            one = jnp.tanh(smooth * w_first + wide_columns(columns[1], width))
            one_slope = (1.0 - one * one) * w_first
            low = jnp.concatenate([one.astype(bf16), one_slope.astype(bf16)], axis=1)
            product = dot(w_embed_t[...], low)
            two = jnp.tanh(product[:, 0:width] + wide_columns(columns[2], width))
            both = one + two
            total = both.astype(bf16)
            second[b * blocks + i] = total
            slope[b * blocks + i] = (one_slope + (1.0 - two * two) * product[:, width:]).astype(bf16)
            spread = jnp.concatenate(
                [jnp.where(segment, radial[x, i, b : b + 1, :], 0.0) for x in range(4)], axis=0
            )
            high = spread.astype(bf16)
            halves = jnp.concatenate([high, (spread - high.astype(f32)).astype(bf16)], axis=0)
            part = dot_nt(halves, total)
            rest = dot_nt(high, (both - total.astype(f32)).astype(bf16))
            part = (part[0 : 4 * GROUP, :] + part[4 * GROUP :, :] + rest) * (1.0 / listed)
            start = pl.multiple_of(b * atoms + GROUP * i, GROUP)
            for x in range(4):
                moment[x, pl.ds(start, GROUP), :] = part[x * GROUP : (x + 1) * GROUP, :]
        return carry

    lax.fori_loop(0, blocks, embed, 0)

    for x in range(4):
        moment_t[x] = jnp.transpose(moment[x])
    def describe(e, carry):
        mine = [moment_t[x, pl.ds(pl.multiple_of(e * 8, 8), 8), :] for x in range(4)]
        for f in range(0, AXIS, 2):
            values = []
            for g in (f, f + 1):
                value = mine[0] * moment_t[0, g : g + 1, :]
                for x in range(1, 4):
                    value += mine[x] * moment_t[x, g : g + 1, :]
                values.append(value)
            at = pl.ds(pl.multiple_of(e * 8 * AXIS + f * 8, 16), 16)
            desc[at, :] = jnp.concatenate(values, axis=0).astype(bf16)
        return carry

    lax.fori_loop(0, emb // 8, describe, 0)
    many = beads * atoms
    bias, bias2, out_col = (wide_columns(fit_columns[at], many) for at in range(3))
    hidden = jnp.tanh(dot(cols_here[...], desc[...]) + bias)
    more = jnp.tanh(dot(w2_t[...], hidden.astype(bf16)) + bias2)
    d_more = out_col * (1.0 - more * more)
    d_hidden = out_col + split_dot(w2_here[...], d_more).astype(bf16).astype(f32)
    d_pre = d_hidden * (1.0 - hidden * hidden)
    d_desc[...] = split_dot(rows_here[...], d_pre).astype(bf16).astype(f32)

    def left(e, carry):
        rows = pl.ds(pl.multiple_of(e * 8, 8), 8)
        sums = [None] * 4
        for f in range(AXIS):
            grad = d_desc[pl.ds(pl.multiple_of((e * AXIS + f) * 8, 8), 8), :]
            for x in range(4):
                term = grad * moment_t[x, f : f + 1, :]
                sums[x] = term if f == 0 else sums[x] + term
        for x in range(4):
            d_moment_t[x, rows, :] = sums[x]
        return carry

    lax.fori_loop(0, emb // 8, left, 0)
    for f in range(AXIS):
        terms = [None] * 4
        for e in range(emb // 8):
            grad = d_desc[(e * AXIS + f) * 8 : (e * AXIS + f + 1) * 8, :]
            for x in range(4):
                term = grad * moment_t[x, e * 8 : (e + 1) * 8, :]
                terms[x] = term if e == 0 else terms[x] + term
        for x in range(4):
            d_moment_t[x, f : f + 1, :] += jnp.sum(terms[x], axis=0, keepdims=True)
    for x in range(4):
        d_moment[x] = jnp.transpose(d_moment_t[x]) * (1.0 / listed)

    row_of = lax.broadcasted_iota(jnp.int32, (atoms, width), 0)
    lane_of = lax.broadcasted_iota(jnp.int32, (atoms, width), 1)

    def backward(i, carry):
        for b in range(beads):
            start = pl.multiple_of(b * atoms + GROUP * i, GROUP)
            left_side = jnp.concatenate(
                [d_moment[x, pl.ds(start, GROUP), :] for x in range(4)], axis=0
            )
            high = left_side.astype(bf16)
            halves = jnp.concatenate([high, (left_side - high.astype(f32)).astype(bf16)], axis=0)
            by_second = dot(halves, second[b * blocks + i])
            by_second = by_second[0 : 4 * GROUP, :] + by_second[4 * GROUP :, :]
            by_slope = dot(halves, slope[b * blocks + i])
            by_slope = by_slope[0 : 4 * GROUP, :] + by_slope[4 * GROUP :, :]
            along = None
            for x in range(4):
                rows = slice(x * GROUP, (x + 1) * GROUP)
                pair_grad[x, b : b + 1, :] = jnp.sum(
                    jnp.where(segment, by_second[rows, :], 0.0), axis=0, keepdims=True
                )
                term = by_slope[rows, :] * radial[x, i, b : b + 1, :]
                along = term if along is None else along + term
            pair_grad[4, b : b + 1, :] = jnp.sum(
                jnp.where(segment, along, 0.0), axis=0, keepdims=True
            )
        inv = inverse[i]
        smooth = radial[0, i]
        offs = [offset[c, i] for c in range(comps)]
        along = pair_grad[1] * offs[0] + pair_grad[2] * offs[1] + pair_grad[3] * offs[2]
        live = jnp.where(smooth > 0.0, 1.0, 0.0)
        d_inv = live * (pair_grad[0] + pair_grad[4]) + 2.0 * smooth * along
        pull = d_inv * inv * inv * inv
        scaled = smooth * inv
        grads = [pair_grad[c + 1] * scaled - pull * offs[c] for c in range(comps)]
        high = [g.astype(bf16) for g in grads]
        low = [(g - h.astype(f32)) for g, h in zip(grads, high)]
        sides = jnp.concatenate(
            [h.astype(f32) for h in high] + low, axis=0
        ).astype(bf16)
        ix = index[i, 0:1, :]
        for j in range(len(sources)):
            hot = jnp.where(row_of == ix - j * LANES, 1.0, 0.0)
            if j == 0:
                hot = hot - jnp.where(row_of == GROUP * i + lane_of // listed, 1.0, 0.0)
            totals[j * LANES : j * LANES + atoms, 0 : 6 * 8] += dot_nt(hot.astype(bf16), sides)
        return carry

    lax.fori_loop(0, blocks, backward, 0)

    targets = ((own_f, 0), (near_f, 0), (link_f, 0), (link_f, rows), (near_f, rows))
    for j, (out, at) in enumerate(targets):
        turned = jnp.transpose(totals[j * LANES : (j + 1) * LANES, :])
        whole = turned[0:24, :] + turned[24:48, :]
        for c in range(comps):
            value = -whole[c * 8 : c * 8 + beads, 0:atoms]
            if j == 0:
                value = mom[c] + (time_step * force_gain) * value
            out[at + c * beads : at + (c + 1) * beads, :] = value


def finish_kernel(own, kicked, near, link, far, maps, *outs_and_scratch):
    outs, stacked = outs_and_scratch[:-1], outs_and_scratch[-1]
    rows, atoms = kicked.shape
    force = near[0:rows, :] + (link[0:rows, :] + far[rows : 2 * rows, :])
    stacked[...] = jnp.zeros_like(stacked)
    stacked[0:rows, 0:atoms] = own[0:rows, :]
    stacked[rows : 2 * rows, 0:atoms] = kicked[...] + force * (time_step * force_gain)
    shares = jnp.dot(
        maps[lax.axis_index("bead")],
        stacked[...],
        precision=lax.Precision.HIGHEST,
        preferred_element_type=f32,
    )
    for at, out in enumerate(outs):
        for k in range(out.shape[0]):
            start = at * 2 * rows + k * out.shape[1]
            out[k] = shares[start : start + out.shape[1], 0:atoms]


def on_device(
    positions, momenta, neighbours, nbr_count, send_rows, embed_first, embed_weight,
    embed_bias, fit_weight, fit_bias, fit_weight2, fit_bias2, fit_out,
):
    bead_dev, comps, atoms = positions.shape
    listed = neighbours.shape[1]
    wide, fit = fit_weight.shape
    emb = embed_weight.shape[0]
    fit_pad = -(-fit // LANES) * LANES
    rows = bead_dev * comps
    blocks = atoms // GROUP
    width = GROUP * listed
    many = bead_dev * atoms
    shape = jax.ShapeDtypeStruct
    big = pltpu.CompilerParams(vmem_limit_bytes=44 * 1024 * 1024)
    small = pltpu.CompilerParams(vmem_limit_bytes=4 * 1024 * 1024)

    vmem = pl.BlockSpec(memory_space=pltpu.VMEM)

    domains = lax.axis_size("space")
    pairs = [(d, d + 1) for d in range(0, domains - 1, 2)]
    links = [(d, d + 1) for d in range(1, domains - 1, 2)]

    def swapped(value, which):
        return lax.ppermute(value, "space", which + [(b, a) for a, b in which])

    send_blocks = send_rows.shape[1]
    own = pl.pallas_call(
        pack_kernel,
        out_shape=shape((rows + send_blocks, atoms), f32),
        in_specs=[vmem] * 2,
        out_specs=vmem,
        compiler_params=small,
        name="pack",
    )(positions.transpose(1, 0, 2), send_rows)
    core = swapped(own, pairs)
    link = swapped(jnp.concatenate([own, core], axis=0), links)
    far = swapped(link, pairs)

    own_f, near_f, link_f = pl.pallas_call(
        force_kernel,
        out_shape=[shape((rows, atoms), f32), shape((2 * rows, atoms), f32), shape((2 * rows, atoms), f32)],
        in_specs=[vmem] * 15,
        out_specs=[vmem] * 3,
        scratch_shapes=[
            pltpu.VMEM((5, comps, 8, LANES), f32),
            pltpu.VMEM((8, LANES), jnp.int32),
            pltpu.VMEM((4, 8, LANES), jnp.int32),
            pltpu.VMEM((4, blocks, 8, width), f32),
            pltpu.VMEM((blocks, 8, width), f32),
            pltpu.VMEM((comps, blocks, 8, width), f32),
            pltpu.VMEM((bead_dev * blocks, emb, width), bf16),
            pltpu.VMEM((bead_dev * blocks, emb, width), bf16),
            pltpu.VMEM((4, many, emb), f32),
            pltpu.VMEM((4, emb, many), f32),
            pltpu.VMEM((wide, many), bf16),
            pltpu.VMEM((wide, many), f32),
            pltpu.VMEM((4, emb, many), f32),
            pltpu.VMEM((4, many, emb), f32),
            pltpu.VMEM((5, 8, width), f32),
            pltpu.VMEM((5 * LANES, LANES), f32),
            pltpu.VMEM((blocks, 8, width), jnp.int32),
            pltpu.VMEM((wide, fit_pad), bf16),
            pltpu.VMEM((fit_pad, wide), bf16),
            pltpu.VMEM((emb, emb), bf16),
            pltpu.VMEM((fit_pad, fit_pad), bf16),
            pltpu.VMEM((fit_pad, fit_pad), bf16),
            pltpu.VMEM((3, emb, LANES), f32),
            pltpu.VMEM((3, fit_pad, LANES), f32),
        ],
        compiler_params=big,
        name="forces",
    )(
        own, momenta.transpose(1, 0, 2), core, link, far, neighbours.reshape(blocks, width), nbr_count.reshape(1, atoms),
        embed_first, embed_weight, embed_bias.reshape(1, emb), fit_weight.T,
        fit_bias.reshape(1, fit), fit_weight2, fit_bias2.reshape(1, fit), fit_out.reshape(1, fit),
    )
    near = swapped(near_f, pairs)
    link = swapped(
        jnp.concatenate([link_f[:rows] + near[rows:], link_f[rows:]], axis=0), links
    )
    far = swapped(link, pairs)

    groups = lax.axis_size("bead")
    maps = jnp.asarray(propagation_table(groups, bead_dev))
    shares = pl.pallas_call(
        finish_kernel,
        out_shape=[shape((2 * comps, bead_dev, atoms), f32)] * groups,
        in_specs=[vmem] * 6,
        out_specs=[vmem] * groups,
        scratch_shapes=[pltpu.VMEM((LANES, LANES), f32)],
        compiler_params=small,
        name="propagate",
    )(own, own_f, near, link, far, maps)
    if groups == 2:
        result = shares[0] + lax.ppermute(shares[1], "bead", [(0, 1), (1, 0)])
    else:
        parts = lax.all_to_all(jnp.stack(shares), "bead", split_axis=0, concat_axis=0, tiled=True)
        result = parts.sum(axis=0)
    return (result[:comps].transpose(1, 0, 2), result[comps:].transpose(1, 0, 2))


def solution(mesh):
    in_specs = (
        P("bead", None, "space"),
        P("bead", None, "space"),
        P("space", None),
        P("space"),
        P("space", None, None),
    ) + (P(),) * 8
    out_specs = (P("bead", None, "space"), P("bead", None, "space"))
    return jax.shard_map(
        on_device, mesh=mesh, in_specs=in_specs, out_specs=out_specs, check_vma=False
    )
```

```python
import functools

import jax
import jax.numpy as jnp
import numpy as np
from jax import lax
from jax.experimental import pallas as pl
from jax.experimental.pallas import tpu as pltpu
from jax.sharding import PartitionSpec as P

AXIS = 16
LANES = 128
GROUP = 8

cycle_freq = 0.5
time_step = 1.0
soften = 0.25
force_gain = 64.0

f32 = jnp.float32
bf16 = jnp.bfloat16


def passed_along(value, axis, steps):
    count = lax.axis_size(axis)
    first, last = (max(0, -steps), min(count, count - steps))
    return lax.ppermute(value, axis, [(source, source + steps) for source in range(first, last)])


def mode_maps(beads):
    column = np.arange(beads)[None, :]
    bead_row = np.arange(beads)[:, None]
    phases = 2.0 * np.pi * bead_row * column / beads
    mode_basis = np.where(
        column == 0,
        1.0 / np.sqrt(beads),
        np.where(
            2 * column < beads,
            np.sqrt(2.0 / beads) * np.cos(phases),
            np.where(
                2 * column == beads,
                np.cos(phases) / np.sqrt(beads),
                np.sqrt(2.0 / beads) * np.sin(phases),
            ),
        ),
    )
    frequency = 2.0 * cycle_freq * np.sin(np.pi * np.arange(beads) / beads)
    angles = frequency * time_step
    safe_freq = np.where(frequency > 0, frequency, 1.0)
    cosine = np.cos(angles)
    drift = np.where(frequency > 0, np.sin(angles) / safe_freq, time_step)
    pull = -frequency * np.sin(angles)
    keep_map = mode_basis * cosine[None, :] @ mode_basis.T
    drift_map = mode_basis * drift[None, :] @ mode_basis.T
    pull_map = mode_basis * pull[None, :] @ mode_basis.T
    return keep_map, drift_map, pull_map


def propagation_table(groups, bead_dev):
    keep, drift, pull = mode_maps(groups * bead_dev)
    table = np.zeros((groups, groups, 2, 3, bead_dev, 2, 3, bead_dev))
    for source in range(groups):
        cols = slice(source * bead_dev, (source + 1) * bead_dev)
        for target in range(groups):
            rows = slice(target * bead_dev, (target + 1) * bead_dev)
            for c in range(3):
                table[source, target, 0, c, :, 0, c, :] = keep[rows, cols]
                table[source, target, 0, c, :, 1, c, :] = drift[rows, cols]
                table[source, target, 1, c, :, 0, c, :] = pull[rows, cols]
                table[source, target, 1, c, :, 1, c, :] = keep[rows, cols]
    if groups == 2:
        table[1] = table[1, ::-1].copy()
    table = table.reshape(groups, groups * 6 * bead_dev, 6 * bead_dev)
    return np.pad(table, ((0, 0), (0, 0), (0, LANES - table.shape[2]))).astype(np.float32)


def lane_take(values, picked):
    numbers = lax.GatherDimensionNumbers(
        offset_dims=(),
        collapsed_slice_dims=(1,),
        start_index_map=(1,),
        operand_batching_dims=(0,),
        start_indices_batching_dims=(0,),
    )
    return lax.gather(
        values,
        picked[..., None],
        numbers,
        (1, 1),
        mode=lax.GatherScatterMode.PROMISE_IN_BOUNDS,
    )


def dot(a, b):
    return jnp.dot(a, b, preferred_element_type=f32)


def dot_nt(a, b):
    return lax.dot_general(a, b, (((1,), (1,)), ((), ())), preferred_element_type=f32)


def column_of(row, rows):
    wide = jnp.broadcast_to(row, (LANES, rows))
    return jnp.transpose(wide)


def wide_columns(column, width):
    return jnp.concatenate([column] * (width // LANES), axis=1)


def split_dot(a, b):
    high = b.astype(bf16)
    return dot(a, high) + dot(a, (b - high.astype(f32)).astype(bf16))


def pack_kernel(pos, send, out):
    comps, beads, _ = pos.shape
    for c in range(comps):
        out[c * beads : (c + 1) * beads, :] = pos[c]
    out[comps * beads : comps * beads + send.shape[1], :] = send[0].astype(f32)


def unit(n):
    same = lax.broadcasted_iota(jnp.int32, (n, n), 0) == lax.broadcasted_iota(jnp.int32, (n, n), 1)
    return jnp.where(same, 1.0, 0.0).astype(bf16)


def force_kernel(
    own, mom, core, link, far, idx, cnt, first, w_embed, e_bias, fit_t, f_bias, fit_w2, f_bias2, f_out,
    own_f, near_f, link_f,
    table, counts, sent, radial, inverse, offset, second, slope,
    moment, moment_t, desc, d_desc, d_moment_t, d_moment, pair_grad, totals, index,
    rows_here, cols_here, w_embed_t, w2_here, w2_t, columns, fit_columns,
):
    beads = 4
    comps = 3
    atoms = own.shape[1]
    blocks, width = idx.shape
    listed = width // GROUP
    emb = w_embed.shape[0]
    fit, wide = fit_t.shape
    fit_pad = rows_here.shape[1]
    rows = beads * comps
    odd = lax.rem(lax.axis_index("space"), 2) == 1
    block_of = ((2, 1), (1, 2), (0, 3), (3, 0))
    table[...] = jnp.zeros_like(table)
    sent[...] = jnp.zeros_like(sent)
    sources = ((own, 0), (core, 0), (link, 0), (link, link.shape[0] // 2), (far, 0))
    for role, (source, at) in enumerate(sources):
        for c in range(comps):
            table[role, c, 0:beads, 0:atoms] = source[at + c * beads : at + (c + 1) * beads, :]
        if role > 0:
            if_odd, if_even = (
                source[at + rows + j : at + rows + j + 1, :] for j in block_of[role - 1]
            )
            row = jnp.maximum(jnp.where(odd, if_odd, if_even), 0.0).astype(jnp.int32)
            sent[role - 1, :, 0:atoms] = jnp.broadcast_to(row, (8, atoms))
    role_of = [
        jnp.where(odd, 1 + [pair[0] for pair in block_of].index(j), 1 + [pair[1] for pair in block_of].index(j))
        for j in range(4)
    ]
    counts[...] = jnp.zeros_like(counts)
    counts[:, 0:atoms] = jnp.broadcast_to(cnt[...], (8, atoms))
    pair_grad[...] = jnp.zeros_like(pair_grad)
    totals[...] = jnp.zeros_like(totals)
    for i in range(blocks):
        index[i] = jnp.broadcast_to(idx[i : i + 1, :], (8, width))

    columns[0] = column_of(first[0:1, :], emb)
    columns[1] = column_of(first[1:2, :], emb)
    columns[2] = column_of(e_bias[...], emb)
    for at, vector in enumerate((f_bias, f_bias2, f_out)):
        pad = jnp.zeros((1, fit_pad - fit), f32)
        fit_columns[at] = column_of(jnp.concatenate([vector[...], pad], axis=1), fit_pad)
    w_embed_t[...] = dot_nt(unit(emb), w_embed[...]).astype(bf16)
    w2_here[...] = jnp.zeros_like(w2_here)
    w2_here[0:fit, 0:fit] = fit_w2[...]
    w2_t[...] = dot_nt(unit(fit_pad), w2_here[...]).astype(bf16)
    cols_here[fit:fit_pad, :] = jnp.zeros((fit_pad - fit, wide), bf16)
    row = lax.broadcasted_iota(jnp.int32, (LANES, LANES), 0)
    source = AXIS * (row % 8) + row // 8
    order = jnp.where(lax.broadcasted_iota(jnp.int32, (LANES, LANES), 1) == source, 1.0, 0.0).astype(bf16)
    blank = jnp.zeros((LANES, fit_pad - fit), f32)
    chunks = wide // LANES
    each = -(-chunks // blocks)

    lane = lax.broadcasted_iota(jnp.int32, (8, LANES), 1)

    def pairs(i, carry):
        for turn in range(each):
            chunk = jnp.minimum(each * i + turn, chunks - 1)
            part = pl.ds(pl.multiple_of(chunk * LANES, LANES), LANES)
            chunk_t = fit_t[:, part]
            rows_here[part, :] = jnp.concatenate([dot_nt(order, chunk_t), blank], axis=1).astype(bf16)
            cols_here[0:fit, part] = dot_nt(chunk_t, order).astype(bf16)
        for part in range(width // LANES):
            cols = slice(part * LANES, (part + 1) * LANES)
            ix = index[i, :, cols]
            atom = GROUP * i + part * (LANES // listed) + lane // listed
            entry = lane % listed
            role = jnp.where(ix >= atoms, role_of[0], 0)
            block = jnp.where(ix >= atoms, 1, 0)
            for j in range(1, 4):
                role = jnp.where(ix >= (j + 1) * atoms, role_of[j], role)
                block = jnp.where(ix >= (j + 1) * atoms, j + 1, block)
            slot = ix - atoms * block
            local = slot
            for r in range(1, 5):
                local = jnp.where(role == r, lane_take(sent[r - 1], slot), local)
            index[i, :, cols] = local + role * LANES
            active = entry < lane_take(counts[...], atom)
            offs = []
            for c in range(comps):
                near = lane_take(table[0, c], local)
                for j in range(1, len(sources)):
                    near = jnp.where(role == j, lane_take(table[j, c], local), near)
                offs.append(near - lane_take(table[0, c], atom))
            square = offs[0] * offs[0] + offs[1] * offs[1] + offs[2] * offs[2]
            inv = lax.rsqrt(square + soften)
            smooth = jnp.where(active, inv, 0.0)
            scaled = smooth * inv
            inverse[i, :, cols] = inv
            radial[0, i, :, cols] = smooth
            for c in range(comps):
                offset[c, i, :, cols] = offs[c]
                radial[c + 1, i, :, cols] = scaled * offs[c]
        return carry

    lax.fori_loop(0, blocks, pairs, 0)

    segment = (
        lax.broadcasted_iota(jnp.int32, (GROUP, width), 1) // listed
        == lax.broadcasted_iota(jnp.int32, (GROUP, width), 0)
    )

    def embed(i, carry):
        for b in range(beads):
            totals_here, rests = [], []
            for at in range(0, width, 2 * LANES):
                cols = slice(at, at + 2 * LANES)
                w_first = wide_columns(columns[0], 2 * LANES)
                one = jnp.tanh(radial[0, i, b : b + 1, cols] * w_first + wide_columns(columns[1], 2 * LANES))
                one_slope = (1.0 - one * one) * w_first
                low = jnp.concatenate([one.astype(bf16), one_slope.astype(bf16)], axis=1)
                product = dot(w_embed_t[...], low)
                two = jnp.tanh(product[:, 0 : 2 * LANES] + wide_columns(columns[2], 2 * LANES))
                both = one + two
                totals_here.append(both.astype(bf16))
                rests.append((both - totals_here[-1].astype(f32)).astype(bf16))
                second[b * blocks + i, :, cols] = totals_here[-1]
                slope[b * blocks + i, :, cols] = (one_slope + (1.0 - two * two) * product[:, 2 * LANES :]).astype(bf16)
            total = jnp.concatenate(totals_here, axis=1)
            spread = jnp.concatenate(
                [jnp.where(segment, radial[x, i, b : b + 1, :], 0.0) for x in range(4)], axis=0
            )
            high = spread.astype(bf16)
            halves = jnp.concatenate([high, (spread - high.astype(f32)).astype(bf16)], axis=0)
            part = dot_nt(halves, total)
            rest = dot_nt(high, jnp.concatenate(rests, axis=1))
            part = (part[0 : 4 * GROUP, :] + part[4 * GROUP :, :] + rest) * (1.0 / listed)
            start = pl.multiple_of(b * atoms + GROUP * i, GROUP)
            for x in range(4):
                moment[x, pl.ds(start, GROUP), :] = part[x * GROUP : (x + 1) * GROUP, :]
        return carry

    lax.fori_loop(0, blocks, embed, 0)

    for x in range(4):
        moment_t[x] = jnp.transpose(moment[x])
    def describe(e, carry):
        mine = [moment_t[x, pl.ds(pl.multiple_of(e * 8, 8), 8), :] for x in range(4)]
        for f in range(0, AXIS, 2):
            values = []
            for g in (f, f + 1):
                value = mine[0] * moment_t[0, g : g + 1, :]
                for x in range(1, 4):
                    value += mine[x] * moment_t[x, g : g + 1, :]
                values.append(value)
            at = pl.ds(pl.multiple_of(e * 8 * AXIS + f * 8, 16), 16)
            desc[at, :] = jnp.concatenate(values, axis=0).astype(bf16)
        return carry

    lax.fori_loop(0, emb // 8, describe, 0)
    many = beads * atoms
    bias, bias2, out_col = (wide_columns(fit_columns[at], many) for at in range(3))
    hidden = jnp.tanh(dot(cols_here[...], desc[...]) + bias)
    more = jnp.tanh(dot(w2_t[...], hidden.astype(bf16)) + bias2)
    d_more = out_col * (1.0 - more * more)
    d_hidden = out_col + split_dot(w2_here[...], d_more).astype(bf16).astype(f32)
    d_pre = d_hidden * (1.0 - hidden * hidden)
    d_desc[...] = split_dot(rows_here[...], d_pre).astype(bf16).astype(f32)

    def left(e, carry):
        rows = pl.ds(pl.multiple_of(e * 8, 8), 8)
        sums = [None] * 4
        for f in range(AXIS):
            grad = d_desc[pl.ds(pl.multiple_of((e * AXIS + f) * 8, 8), 8), :]
            for x in range(4):
                term = grad * moment_t[x, f : f + 1, :]
                sums[x] = term if f == 0 else sums[x] + term
        for x in range(4):
            d_moment_t[x, rows, :] = sums[x]
        return carry

    lax.fori_loop(0, emb // 8, left, 0)
    for f in range(AXIS):
        terms = [None] * 4
        for e in range(emb // 8):
            grad = d_desc[(e * AXIS + f) * 8 : (e * AXIS + f + 1) * 8, :]
            for x in range(4):
                term = grad * moment_t[x, e * 8 : (e + 1) * 8, :]
                terms[x] = term if e == 0 else terms[x] + term
        for x in range(4):
            d_moment_t[x, f : f + 1, :] += jnp.sum(terms[x], axis=0, keepdims=True)
    for x in range(4):
        d_moment[x] = jnp.transpose(d_moment_t[x]) * (1.0 / listed)

    row_of = lax.broadcasted_iota(jnp.int32, (atoms, width), 0).astype(jnp.int16)
    lane_of = lax.broadcasted_iota(jnp.int32, (1, width), 1)

    def backward(i, carry):
        for b in range(beads):
            start = pl.multiple_of(b * atoms + GROUP * i, GROUP)
            left_side = jnp.concatenate(
                [d_moment[x, pl.ds(start, GROUP), :] for x in range(4)], axis=0
            )
            high = left_side.astype(bf16)
            halves = jnp.concatenate([high, (left_side - high.astype(f32)).astype(bf16)], axis=0)
            by_second = dot(halves, second[b * blocks + i])
            by_second = by_second[0 : 4 * GROUP, :] + by_second[4 * GROUP :, :]
            by_slope = dot(halves, slope[b * blocks + i])
            by_slope = by_slope[0 : 4 * GROUP, :] + by_slope[4 * GROUP :, :]
            along = None
            for x in range(4):
                rows = slice(x * GROUP, (x + 1) * GROUP)
                pair_grad[x, b : b + 1, :] = jnp.sum(
                    jnp.where(segment, by_second[rows, :], 0.0), axis=0, keepdims=True
                )
                term = by_slope[rows, :] * radial[x, i, b : b + 1, :]
                along = term if along is None else along + term
            pair_grad[4, b : b + 1, :] = jnp.sum(
                jnp.where(segment, along, 0.0), axis=0, keepdims=True
            )
        inv = inverse[i]
        smooth = radial[0, i]
        offs = [offset[c, i] for c in range(comps)]
        along = pair_grad[1] * offs[0] + pair_grad[2] * offs[1] + pair_grad[3] * offs[2]
        live = jnp.where(smooth > 0.0, 1.0, 0.0)
        d_inv = live * (pair_grad[0] + pair_grad[4]) + 2.0 * smooth * along
        pull = d_inv * inv * inv * inv
        scaled = smooth * inv
        grads = [pair_grad[c + 1] * scaled - pull * offs[c] for c in range(comps)]
        high = [g.astype(bf16) for g in grads]
        low = [(g - h.astype(f32)) for g, h in zip(grads, high)]
        sides = jnp.concatenate(
            [h.astype(f32) for h in high] + low, axis=0
        ).astype(bf16)
        ix = index[i, 0:1, :]
        for j in range(len(sources)):
            one, none = jnp.ones((), bf16), jnp.zeros((), bf16)
            hot = jnp.where(row_of == (ix - j * LANES).astype(jnp.int16), one, none)
            if j == 0:
                centre = (GROUP * i + lane_of // listed).astype(jnp.int16)
                hot = hot - jnp.where(row_of == centre, one, none)
            totals[j * LANES : j * LANES + atoms, 0 : 6 * 8] += dot_nt(hot, sides)
        return carry

    lax.fori_loop(0, blocks, backward, 0, unroll=2)

    targets = ((own_f, 0), (near_f, 0), (link_f, 0), (link_f, rows), (near_f, rows))
    for j, (out, at) in enumerate(targets):
        turned = jnp.transpose(totals[j * LANES : (j + 1) * LANES, :])
        whole = turned[0:24, :] + turned[24:48, :]
        for c in range(comps):
            value = -whole[c * 8 : c * 8 + beads, 0:atoms]
            if j == 0:
                value = mom[c] + (time_step * force_gain) * value
            out[at + c * beads : at + (c + 1) * beads, :] = value


def finish_kernel(own, kicked, near, link, far, maps, *outs_and_scratch):
    outs, stacked = outs_and_scratch[:-1], outs_and_scratch[-1]
    rows, atoms = kicked.shape
    force = near[0:rows, :] + (link[0:rows, :] + far[rows : 2 * rows, :])
    stacked[...] = jnp.zeros_like(stacked)
    stacked[0:rows, 0:atoms] = own[0:rows, :]
    stacked[rows : 2 * rows, 0:atoms] = kicked[...] + force * (time_step * force_gain)
    shares = jnp.dot(
        maps[lax.axis_index("bead")],
        stacked[...],
        precision=lax.Precision.HIGHEST,
        preferred_element_type=f32,
    )
    for at, out in enumerate(outs):
        for k in range(out.shape[0]):
            start = at * 2 * rows + k * out.shape[1]
            out[k] = shares[start : start + out.shape[1], 0:atoms]


def on_device(
    positions, momenta, neighbours, nbr_count, send_rows, embed_first, embed_weight,
    embed_bias, fit_weight, fit_bias, fit_weight2, fit_bias2, fit_out,
):
    bead_dev, comps, atoms = positions.shape
    listed = neighbours.shape[1]
    wide, fit = fit_weight.shape
    emb = embed_weight.shape[0]
    fit_pad = -(-fit // LANES) * LANES
    rows = bead_dev * comps
    blocks = atoms // GROUP
    width = GROUP * listed
    many = bead_dev * atoms
    shape = jax.ShapeDtypeStruct
    big = pltpu.CompilerParams(vmem_limit_bytes=44 * 1024 * 1024)
    small = pltpu.CompilerParams(vmem_limit_bytes=4 * 1024 * 1024)

    vmem = pl.BlockSpec(memory_space=pltpu.VMEM)

    domains = lax.axis_size("space")
    pairs = [(d, d + 1) for d in range(0, domains - 1, 2)]
    links = [(d, d + 1) for d in range(1, domains - 1, 2)]

    def swapped(value, which):
        return lax.ppermute(value, "space", which + [(b, a) for a, b in which])

    send_blocks = send_rows.shape[1]
    own = pl.pallas_call(
        pack_kernel,
        out_shape=shape((rows + send_blocks, atoms), f32),
        in_specs=[vmem] * 2,
        out_specs=vmem,
        compiler_params=small,
        name="pack",
    )(positions.transpose(1, 0, 2), send_rows)
    core = swapped(own, pairs)
    link = swapped(jnp.concatenate([own, core], axis=0), links)
    far = swapped(link, pairs)

    own_f, near_f, link_f = pl.pallas_call(
        force_kernel,
        out_shape=[shape((rows, atoms), f32), shape((2 * rows, atoms), f32), shape((2 * rows, atoms), f32)],
        in_specs=[vmem] * 15,
        out_specs=[vmem] * 3,
        scratch_shapes=[
            pltpu.VMEM((5, comps, 8, LANES), f32),
            pltpu.VMEM((8, LANES), jnp.int32),
            pltpu.VMEM((4, 8, LANES), jnp.int32),
            pltpu.VMEM((4, blocks, 8, width), f32),
            pltpu.VMEM((blocks, 8, width), f32),
            pltpu.VMEM((comps, blocks, 8, width), f32),
            pltpu.VMEM((bead_dev * blocks, emb, width), bf16),
            pltpu.VMEM((bead_dev * blocks, emb, width), bf16),
            pltpu.VMEM((4, many, emb), f32),
            pltpu.VMEM((4, emb, many), f32),
            pltpu.VMEM((wide, many), bf16),
            pltpu.VMEM((wide, many), f32),
            pltpu.VMEM((4, emb, many), f32),
            pltpu.VMEM((4, many, emb), f32),
            pltpu.VMEM((5, 8, width), f32),
            pltpu.VMEM((5 * LANES, LANES), f32),
            pltpu.VMEM((blocks, 8, width), jnp.int32),
            pltpu.VMEM((wide, fit_pad), bf16),
            pltpu.VMEM((fit_pad, wide), bf16),
            pltpu.VMEM((emb, emb), bf16),
            pltpu.VMEM((fit_pad, fit_pad), bf16),
            pltpu.VMEM((fit_pad, fit_pad), bf16),
            pltpu.VMEM((3, emb, LANES), f32),
            pltpu.VMEM((3, fit_pad, LANES), f32),
        ],
        compiler_params=big,
        name="forces",
    )(
        own, momenta.transpose(1, 0, 2), core, link, far, neighbours.reshape(blocks, width), nbr_count.reshape(1, atoms),
        embed_first, embed_weight, embed_bias.reshape(1, emb), fit_weight.T,
        fit_bias.reshape(1, fit), fit_weight2, fit_bias2.reshape(1, fit), fit_out.reshape(1, fit),
    )
    near = swapped(near_f, pairs)
    link = swapped(
        jnp.concatenate([link_f[:rows] + near[rows:], link_f[rows:]], axis=0), links
    )
    far = swapped(link, pairs)

    groups = lax.axis_size("bead")
    maps = jnp.asarray(propagation_table(groups, bead_dev))
    shares = pl.pallas_call(
        finish_kernel,
        out_shape=[shape((2 * comps, bead_dev, atoms), f32)] * groups,
        in_specs=[vmem] * 6,
        out_specs=[vmem] * groups,
        scratch_shapes=[pltpu.VMEM((LANES, LANES), f32)],
        compiler_params=small,
        name="propagate",
    )(own, own_f, near, link, far, maps)
    if groups == 2:
        result = shares[0] + lax.ppermute(shares[1], "bead", [(0, 1), (1, 0)])
    else:
        parts = lax.all_to_all(jnp.stack(shares), "bead", split_axis=0, concat_axis=0, tiled=True)
        result = parts.sum(axis=0)
    return (result[:comps].transpose(1, 0, 2), result[comps:].transpose(1, 0, 2))


def solution(mesh):
    in_specs = (
        P("bead", None, "space"),
        P("bead", None, "space"),
        P("space", None),
        P("space"),
        P("space", None, None),
    ) + (P(),) * 8
    out_specs = (P("bead", None, "space"), P("bead", None, "space"))
    return jax.shard_map(
        on_device, mesh=mesh, in_specs=in_specs, out_specs=out_specs, check_vma=False
    )
```

```python
import functools

import jax
import jax.numpy as jnp
import numpy as np
from jax import lax
from jax.experimental import pallas as pl
from jax.experimental.pallas import tpu as pltpu
from jax.sharding import PartitionSpec as P

AXIS = 16
LANES = 128
GROUP = 8

cycle_freq = 0.5
time_step = 1.0
soften = 0.25
force_gain = 64.0

f32 = jnp.float32
bf16 = jnp.bfloat16


def passed_along(value, axis, steps):
    count = lax.axis_size(axis)
    first, last = (max(0, -steps), min(count, count - steps))
    return lax.ppermute(value, axis, [(source, source + steps) for source in range(first, last)])


def mode_maps(beads):
    column = np.arange(beads)[None, :]
    bead_row = np.arange(beads)[:, None]
    phases = 2.0 * np.pi * bead_row * column / beads
    mode_basis = np.where(
        column == 0,
        1.0 / np.sqrt(beads),
        np.where(
            2 * column < beads,
            np.sqrt(2.0 / beads) * np.cos(phases),
            np.where(
                2 * column == beads,
                np.cos(phases) / np.sqrt(beads),
                np.sqrt(2.0 / beads) * np.sin(phases),
            ),
        ),
    )
    frequency = 2.0 * cycle_freq * np.sin(np.pi * np.arange(beads) / beads)
    angles = frequency * time_step
    safe_freq = np.where(frequency > 0, frequency, 1.0)
    cosine = np.cos(angles)
    drift = np.where(frequency > 0, np.sin(angles) / safe_freq, time_step)
    pull = -frequency * np.sin(angles)
    keep_map = mode_basis * cosine[None, :] @ mode_basis.T
    drift_map = mode_basis * drift[None, :] @ mode_basis.T
    pull_map = mode_basis * pull[None, :] @ mode_basis.T
    return keep_map, drift_map, pull_map


def propagation_table(groups, bead_dev):
    keep, drift, pull = mode_maps(groups * bead_dev)
    table = np.zeros((groups, groups, 2, 3, bead_dev, 2, 3, bead_dev))
    for source in range(groups):
        cols = slice(source * bead_dev, (source + 1) * bead_dev)
        for target in range(groups):
            rows = slice(target * bead_dev, (target + 1) * bead_dev)
            for c in range(3):
                table[source, target, 0, c, :, 0, c, :] = keep[rows, cols]
                table[source, target, 0, c, :, 1, c, :] = drift[rows, cols]
                table[source, target, 1, c, :, 0, c, :] = pull[rows, cols]
                table[source, target, 1, c, :, 1, c, :] = keep[rows, cols]
    if groups == 2:
        table[1] = table[1, ::-1].copy()
    table = table.reshape(groups, groups * 6 * bead_dev, 6 * bead_dev)
    return np.pad(table, ((0, 0), (0, 0), (0, LANES - table.shape[2]))).astype(np.float32)


def lane_take(values, picked):
    numbers = lax.GatherDimensionNumbers(
        offset_dims=(),
        collapsed_slice_dims=(1,),
        start_index_map=(1,),
        operand_batching_dims=(0,),
        start_indices_batching_dims=(0,),
    )
    return lax.gather(
        values,
        picked[..., None],
        numbers,
        (1, 1),
        mode=lax.GatherScatterMode.PROMISE_IN_BOUNDS,
    )


def dot(a, b):
    return jnp.dot(a, b, preferred_element_type=f32)


def dot_nt(a, b):
    return lax.dot_general(a, b, (((1,), (1,)), ((), ())), preferred_element_type=f32)


def column_of(row, rows):
    wide = jnp.broadcast_to(row, (LANES, rows))
    return jnp.transpose(wide)


def wide_columns(column, width):
    return jnp.concatenate([column] * (width // LANES), axis=1)


def split_dot(a, b):
    high = b.astype(bf16)
    return dot(a, high) + dot(a, (b - high.astype(f32)).astype(bf16))


def pack_kernel(pos, send, out):
    comps, beads, _ = pos.shape
    for c in range(comps):
        out[c * beads : (c + 1) * beads, :] = pos[c]
    out[comps * beads : comps * beads + send.shape[1], :] = send[0].astype(f32)


def unit(n):
    same = lax.broadcasted_iota(jnp.int32, (n, n), 0) == lax.broadcasted_iota(jnp.int32, (n, n), 1)
    return jnp.where(same, 1.0, 0.0).astype(bf16)


def force_kernel(
    own, mom, core, link, far, idx, cnt, first, w_embed, e_bias, fit_t, f_bias, fit_w2, f_bias2, f_out,
    own_f, near_f, link_f,
    table, counts, sent, radial, inverse, offset, second, slope,
    moment, moment_t, desc, d_desc, d_moment_t, d_moment, pair_grad, totals, index,
    rows_here, cols_here, w_embed_t, w2_here, w2_t, columns, fit_columns,
):
    beads = 4
    comps = 3
    atoms = own.shape[1]
    blocks, width = idx.shape
    listed = width // GROUP
    emb = w_embed.shape[0]
    fit, wide = fit_t.shape
    fit_pad = rows_here.shape[1]
    rows = beads * comps
    odd = lax.rem(lax.axis_index("space"), 2) == 1
    block_of = ((2, 1), (1, 2), (0, 3), (3, 0))
    table[...] = jnp.zeros_like(table)
    sent[...] = jnp.zeros_like(sent)
    sources = ((own, 0), (core, 0), (link, 0), (link, link.shape[0] // 2), (far, 0))
    for role, (source, at) in enumerate(sources):
        for c in range(comps):
            table[role, c, 0:beads, 0:atoms] = source[at + c * beads : at + (c + 1) * beads, :]
        if role > 0:
            if_odd, if_even = (
                source[at + rows + j : at + rows + j + 1, :] for j in block_of[role - 1]
            )
            row = jnp.maximum(jnp.where(odd, if_odd, if_even), 0.0).astype(jnp.int32)
            sent[role - 1, :, 0:atoms] = jnp.broadcast_to(row, (8, atoms))
    role_of = [
        jnp.where(odd, 1 + [pair[0] for pair in block_of].index(j), 1 + [pair[1] for pair in block_of].index(j))
        for j in range(4)
    ]
    counts[...] = jnp.zeros_like(counts)
    counts[:, 0:atoms] = jnp.broadcast_to(cnt[...], (8, atoms))
    pair_grad[...] = jnp.zeros_like(pair_grad)
    totals[...] = jnp.zeros_like(totals)
    for i in range(blocks):
        index[i] = jnp.broadcast_to(idx[i : i + 1, :], (8, width))

    columns[0] = column_of(first[0:1, :], emb)
    columns[1] = column_of(first[1:2, :], emb)
    columns[2] = column_of(e_bias[...], emb)
    for at, vector in enumerate((f_bias, f_bias2, f_out)):
        pad = jnp.zeros((1, fit_pad - fit), f32)
        fit_columns[at] = column_of(jnp.concatenate([vector[...], pad], axis=1), fit_pad)
    w_embed_t[...] = dot_nt(unit(emb), w_embed[...]).astype(bf16)
    w2_here[...] = jnp.zeros_like(w2_here)
    w2_here[0:fit, 0:fit] = fit_w2[...]
    w2_t[...] = dot_nt(unit(fit_pad), w2_here[...]).astype(bf16)
    cols_here[fit:fit_pad, :] = jnp.zeros((fit_pad - fit, wide), bf16)
    row = lax.broadcasted_iota(jnp.int32, (LANES, LANES), 0)
    source = AXIS * (row % 8) + row // 8
    order = jnp.where(lax.broadcasted_iota(jnp.int32, (LANES, LANES), 1) == source, 1.0, 0.0).astype(bf16)
    blank = jnp.zeros((LANES, fit_pad - fit), f32)
    chunks = wide // LANES
    each = -(-chunks // blocks)

    lane = lax.broadcasted_iota(jnp.int32, (8, LANES), 1)

    def pairs(i, carry):
        for turn in range(each):
            chunk = jnp.minimum(each * i + turn, chunks - 1)
            part = pl.ds(pl.multiple_of(chunk * LANES, LANES), LANES)
            chunk_t = fit_t[:, part]
            rows_here[part, :] = jnp.concatenate([dot_nt(order, chunk_t), blank], axis=1).astype(bf16)
            cols_here[0:fit, part] = dot_nt(chunk_t, order).astype(bf16)
        for part in range(width // LANES):
            cols = slice(part * LANES, (part + 1) * LANES)
            ix = index[i, :, cols]
            atom = GROUP * i + part * (LANES // listed) + lane // listed
            entry = lane % listed
            role = jnp.where(ix >= atoms, role_of[0], 0)
            block = jnp.where(ix >= atoms, 1, 0)
            for j in range(1, 4):
                role = jnp.where(ix >= (j + 1) * atoms, role_of[j], role)
                block = jnp.where(ix >= (j + 1) * atoms, j + 1, block)
            slot = ix - atoms * block
            local = slot
            for r in range(1, 5):
                local = jnp.where(role == r, lane_take(sent[r - 1], slot), local)
            index[i, :, cols] = local + role * LANES
            active = entry < lane_take(counts[...], atom)
            offs = []
            for c in range(comps):
                near = lane_take(table[0, c], local)
                for j in range(1, len(sources)):
                    near = jnp.where(role == j, lane_take(table[j, c], local), near)
                offs.append(near - lane_take(table[0, c], atom))
            square = offs[0] * offs[0] + offs[1] * offs[1] + offs[2] * offs[2]
            inv = lax.rsqrt(square + soften)
            smooth = jnp.where(active, inv, 0.0)
            scaled = smooth * inv
            inverse[i, :, cols] = inv
            radial[0, i, :, cols] = smooth
            for c in range(comps):
                offset[c, i, :, cols] = offs[c]
                radial[c + 1, i, :, cols] = scaled * offs[c]
        return carry

    lax.fori_loop(0, blocks, pairs, 0)

    segment = (
        lax.broadcasted_iota(jnp.int32, (GROUP, width), 1) // listed
        == lax.broadcasted_iota(jnp.int32, (GROUP, width), 0)
    )

    def embed(i, carry):
        for b in range(beads):
            totals_here, rests = [], []
            for at in range(0, width, 2 * LANES):
                cols = slice(at, at + 2 * LANES)
                w_first = wide_columns(columns[0], 2 * LANES)
                one = jnp.tanh(radial[0, i, b : b + 1, cols] * w_first + wide_columns(columns[1], 2 * LANES))
                one_slope = (1.0 - one * one) * w_first
                low = jnp.concatenate([one.astype(bf16), one_slope.astype(bf16)], axis=1)
                product = dot(w_embed_t[...], low)
                two = jnp.tanh(product[:, 0 : 2 * LANES] + wide_columns(columns[2], 2 * LANES))
                both = one + two
                totals_here.append(both.astype(bf16))
                rests.append((both - totals_here[-1].astype(f32)).astype(bf16))
                second[b * blocks + i, :, cols] = totals_here[-1]
                slope[b * blocks + i, :, cols] = (one_slope + (1.0 - two * two) * product[:, 2 * LANES :]).astype(bf16)
            total = jnp.concatenate(totals_here, axis=1)
            spread = jnp.concatenate(
                [jnp.where(segment, radial[x, i, b : b + 1, :], 0.0) for x in range(4)], axis=0
            )
            high = spread.astype(bf16)
            halves = jnp.concatenate([high, (spread - high.astype(f32)).astype(bf16)], axis=0)
            part = dot_nt(halves, total)
            rest = dot_nt(high, jnp.concatenate(rests, axis=1))
            part = (part[0 : 4 * GROUP, :] + part[4 * GROUP :, :] + rest) * (1.0 / listed)
            start = pl.multiple_of(b * atoms + GROUP * i, GROUP)
            for x in range(4):
                moment[x, pl.ds(start, GROUP), :] = part[x * GROUP : (x + 1) * GROUP, :]
        return carry

    lax.fori_loop(0, blocks, embed, 0, unroll=2)

    for x in range(4):
        moment_t[x] = jnp.transpose(moment[x])
    def describe(e, carry):
        mine = [moment_t[x, pl.ds(pl.multiple_of(e * 8, 8), 8), :] for x in range(4)]
        for f in range(0, AXIS, 2):
            values = []
            for g in (f, f + 1):
                value = mine[0] * moment_t[0, g : g + 1, :]
                for x in range(1, 4):
                    value += mine[x] * moment_t[x, g : g + 1, :]
                values.append(value)
            at = pl.ds(pl.multiple_of(e * 8 * AXIS + f * 8, 16), 16)
            desc[at, :] = jnp.concatenate(values, axis=0).astype(bf16)
        return carry

    lax.fori_loop(0, emb // 8, describe, 0)
    many = beads * atoms
    bias, bias2, out_col = (wide_columns(fit_columns[at], many) for at in range(3))
    hidden = jnp.tanh(dot(cols_here[...], desc[...]) + bias)
    more = jnp.tanh(dot(w2_t[...], hidden.astype(bf16)) + bias2)
    d_more = out_col * (1.0 - more * more)
    d_hidden = out_col + split_dot(w2_here[...], d_more).astype(bf16).astype(f32)
    d_pre = d_hidden * (1.0 - hidden * hidden)
    d_desc[...] = split_dot(rows_here[...], d_pre).astype(bf16).astype(f32)

    def left(e, carry):
        rows = pl.ds(pl.multiple_of(e * 8, 8), 8)
        sums = [None] * 4
        for f in range(AXIS):
            grad = d_desc[pl.ds(pl.multiple_of((e * AXIS + f) * 8, 8), 8), :]
            for x in range(4):
                term = grad * moment_t[x, f : f + 1, :]
                sums[x] = term if f == 0 else sums[x] + term
        for x in range(4):
            d_moment_t[x, rows, :] = sums[x]
        return carry

    lax.fori_loop(0, emb // 8, left, 0)
    for f in range(AXIS):
        terms = [None] * 4
        for e in range(emb // 8):
            grad = d_desc[(e * AXIS + f) * 8 : (e * AXIS + f + 1) * 8, :]
            for x in range(4):
                term = grad * moment_t[x, e * 8 : (e + 1) * 8, :]
                terms[x] = term if e == 0 else terms[x] + term
        for x in range(4):
            d_moment_t[x, f : f + 1, :] += jnp.sum(terms[x], axis=0, keepdims=True)
    for x in range(4):
        d_moment[x] = jnp.transpose(d_moment_t[x]) * (1.0 / listed)

    row_of = lax.broadcasted_iota(jnp.int32, (atoms, width), 0).astype(jnp.int16)
    lane_of = lax.broadcasted_iota(jnp.int32, (1, width), 1)

    def backward(i, carry):
        for b in range(beads):
            start = pl.multiple_of(b * atoms + GROUP * i, GROUP)
            left_side = jnp.concatenate(
                [d_moment[x, pl.ds(start, GROUP), :] for x in range(4)], axis=0
            )
            high = left_side.astype(bf16)
            halves = jnp.concatenate([high, (left_side - high.astype(f32)).astype(bf16)], axis=0)
            by_second = dot(halves, second[b * blocks + i])
            by_second = by_second[0 : 4 * GROUP, :] + by_second[4 * GROUP :, :]
            by_slope = dot(halves, slope[b * blocks + i])
            by_slope = by_slope[0 : 4 * GROUP, :] + by_slope[4 * GROUP :, :]
            along = None
            for x in range(4):
                rows = slice(x * GROUP, (x + 1) * GROUP)
                pair_grad[x, b : b + 1, :] = jnp.sum(
                    jnp.where(segment, by_second[rows, :], 0.0), axis=0, keepdims=True
                )
                term = by_slope[rows, :] * radial[x, i, b : b + 1, :]
                along = term if along is None else along + term
            pair_grad[4, b : b + 1, :] = jnp.sum(
                jnp.where(segment, along, 0.0), axis=0, keepdims=True
            )
        inv = inverse[i]
        smooth = radial[0, i]
        offs = [offset[c, i] for c in range(comps)]
        along = pair_grad[1] * offs[0] + pair_grad[2] * offs[1] + pair_grad[3] * offs[2]
        live = jnp.where(smooth > 0.0, 1.0, 0.0)
        d_inv = live * (pair_grad[0] + pair_grad[4]) + 2.0 * smooth * along
        pull = d_inv * inv * inv * inv
        scaled = smooth * inv
        grads = [pair_grad[c + 1] * scaled - pull * offs[c] for c in range(comps)]
        high = [g.astype(bf16) for g in grads]
        low = [(g - h.astype(f32)) for g, h in zip(grads, high)]
        sides = jnp.concatenate(
            [h.astype(f32) for h in high] + low, axis=0
        ).astype(bf16)
        ix = index[i, 0:1, :]
        for j in range(len(sources)):
            one, none = jnp.ones((), bf16), jnp.zeros((), bf16)
            hot = jnp.where(row_of == (ix - j * LANES).astype(jnp.int16), one, none)
            if j == 0:
                centre = (GROUP * i + lane_of // listed).astype(jnp.int16)
                hot = hot - jnp.where(row_of == centre, one, none)
            totals[j * LANES : j * LANES + atoms, 0 : 6 * 8] += dot_nt(hot, sides)
        return carry

    lax.fori_loop(0, blocks, backward, 0, unroll=2)

    targets = ((own_f, 0), (near_f, 0), (link_f, 0), (link_f, rows), (near_f, rows))
    for j, (out, at) in enumerate(targets):
        turned = jnp.transpose(totals[j * LANES : (j + 1) * LANES, :])
        whole = turned[0:24, :] + turned[24:48, :]
        for c in range(comps):
            value = -whole[c * 8 : c * 8 + beads, 0:atoms]
            if j == 0:
                value = mom[c] + (time_step * force_gain) * value
            out[at + c * beads : at + (c + 1) * beads, :] = value


def finish_kernel(own, kicked, near, link, far, maps, *outs_and_scratch):
    outs, stacked = outs_and_scratch[:-1], outs_and_scratch[-1]
    rows, atoms = kicked.shape
    force = near[0:rows, :] + (link[0:rows, :] + far[rows : 2 * rows, :])
    stacked[...] = jnp.zeros_like(stacked)
    stacked[0:rows, 0:atoms] = own[0:rows, :]
    stacked[rows : 2 * rows, 0:atoms] = kicked[...] + force * (time_step * force_gain)
    shares = jnp.dot(
        maps[lax.axis_index("bead")],
        stacked[...],
        precision=lax.Precision.HIGHEST,
        preferred_element_type=f32,
    )
    for at, out in enumerate(outs):
        for k in range(out.shape[0]):
            start = at * 2 * rows + k * out.shape[1]
            out[k] = shares[start : start + out.shape[1], 0:atoms]


def on_device(
    positions, momenta, neighbours, nbr_count, send_rows, embed_first, embed_weight,
    embed_bias, fit_weight, fit_bias, fit_weight2, fit_bias2, fit_out,
):
    bead_dev, comps, atoms = positions.shape
    listed = neighbours.shape[1]
    wide, fit = fit_weight.shape
    emb = embed_weight.shape[0]
    fit_pad = -(-fit // LANES) * LANES
    rows = bead_dev * comps
    blocks = atoms // GROUP
    width = GROUP * listed
    many = bead_dev * atoms
    shape = jax.ShapeDtypeStruct
    big = pltpu.CompilerParams(vmem_limit_bytes=44 * 1024 * 1024)
    small = pltpu.CompilerParams(vmem_limit_bytes=4 * 1024 * 1024)

    vmem = pl.BlockSpec(memory_space=pltpu.VMEM)

    domains = lax.axis_size("space")
    pairs = [(d, d + 1) for d in range(0, domains - 1, 2)]
    links = [(d, d + 1) for d in range(1, domains - 1, 2)]

    def swapped(value, which):
        return lax.ppermute(value, "space", which + [(b, a) for a, b in which])

    send_blocks = send_rows.shape[1]
    own = pl.pallas_call(
        pack_kernel,
        out_shape=shape((rows + send_blocks, atoms), f32),
        in_specs=[vmem] * 2,
        out_specs=vmem,
        compiler_params=small,
        name="pack",
    )(positions.transpose(1, 0, 2), send_rows)
    core = swapped(own, pairs)
    link = swapped(jnp.concatenate([own, core], axis=0), links)
    far = swapped(link, pairs)

    own_f, near_f, link_f = pl.pallas_call(
        force_kernel,
        out_shape=[shape((rows, atoms), f32), shape((2 * rows, atoms), f32), shape((2 * rows, atoms), f32)],
        in_specs=[vmem] * 15,
        out_specs=[vmem] * 3,
        scratch_shapes=[
            pltpu.VMEM((5, comps, 8, LANES), f32),
            pltpu.VMEM((8, LANES), jnp.int32),
            pltpu.VMEM((4, 8, LANES), jnp.int32),
            pltpu.VMEM((4, blocks, 8, width), f32),
            pltpu.VMEM((blocks, 8, width), f32),
            pltpu.VMEM((comps, blocks, 8, width), f32),
            pltpu.VMEM((bead_dev * blocks, emb, width), bf16),
            pltpu.VMEM((bead_dev * blocks, emb, width), bf16),
            pltpu.VMEM((4, many, emb), f32),
            pltpu.VMEM((4, emb, many), f32),
            pltpu.VMEM((wide, many), bf16),
            pltpu.VMEM((wide, many), f32),
            pltpu.VMEM((4, emb, many), f32),
            pltpu.VMEM((4, many, emb), f32),
            pltpu.VMEM((5, 8, width), f32),
            pltpu.VMEM((5 * LANES, LANES), f32),
            pltpu.VMEM((blocks, 8, width), jnp.int32),
            pltpu.VMEM((wide, fit_pad), bf16),
            pltpu.VMEM((fit_pad, wide), bf16),
            pltpu.VMEM((emb, emb), bf16),
            pltpu.VMEM((fit_pad, fit_pad), bf16),
            pltpu.VMEM((fit_pad, fit_pad), bf16),
            pltpu.VMEM((3, emb, LANES), f32),
            pltpu.VMEM((3, fit_pad, LANES), f32),
        ],
        compiler_params=big,
        name="forces",
    )(
        own, momenta.transpose(1, 0, 2), core, link, far, neighbours.reshape(blocks, width), nbr_count.reshape(1, atoms),
        embed_first, embed_weight, embed_bias.reshape(1, emb), fit_weight.T,
        fit_bias.reshape(1, fit), fit_weight2, fit_bias2.reshape(1, fit), fit_out.reshape(1, fit),
    )
    near = swapped(near_f, pairs)
    link = swapped(
        jnp.concatenate([link_f[:rows] + near[rows:], link_f[rows:]], axis=0), links
    )
    far = swapped(link, pairs)

    groups = lax.axis_size("bead")
    maps = jnp.asarray(propagation_table(groups, bead_dev))
    shares = pl.pallas_call(
        finish_kernel,
        out_shape=[shape((2 * comps, bead_dev, atoms), f32)] * groups,
        in_specs=[vmem] * 6,
        out_specs=[vmem] * groups,
        scratch_shapes=[pltpu.VMEM((LANES, LANES), f32)],
        compiler_params=small,
        name="propagate",
    )(own, own_f, near, link, far, maps)
    if groups == 2:
        result = shares[0] + lax.ppermute(shares[1], "bead", [(0, 1), (1, 0)])
    else:
        parts = lax.all_to_all(jnp.stack(shares), "bead", split_axis=0, concat_axis=0, tiled=True)
        result = parts.sum(axis=0)
    return (result[:comps].transpose(1, 0, 2), result[comps:].transpose(1, 0, 2))


def solution(mesh):
    in_specs = (
        P("bead", None, "space"),
        P("bead", None, "space"),
        P("space", None),
        P("space"),
        P("space", None, None),
    ) + (P(),) * 8
    out_specs = (P("bead", None, "space"), P("bead", None, "space"))
    return jax.shard_map(
        on_device, mesh=mesh, in_specs=in_specs, out_specs=out_specs, check_vma=False
    )
```
